256 devices in a mesh: tgt: 8 (over y, x_hi), sup: 32 (over z, x_lo, core).
Axes of the slice: x: 4 (x_hi: 2, x_lo: 2; x = x_hi * 2 + x_lo), y: 4, z: 8, core: 2. Of those that a mesh axis runs over, the one named last changes fastest.
Arguments:
- support: float32 [256, 3, 1024], P(('tgt', 'sup')), may hold values from -6 to 6
- support_labels: int32 [256], replicated, may hold values from 0 to 9
- targets: float32 [256, 3, 1024], P('tgt'), may hold values from -6 to 6
- target_labels: int32 [256], P('tgt'), may hold values from 0 to 9
Outputs:
- support_grad: float32 [256, 3, 1024], P(('tgt', 'sup'))
- objective: float32 [], replicated
The draws below stay inside these ranges and needn't reach their ends.
All inputs are finite; a program needn't handle non-finite values.
Results may differ from the reference program's by a relative error of at most 0.0003.
Values sent between devices are 32-bit elements; how exact they have to be, the bound alone decides.
No kernel may reach another device: no remote copies, remote signals or barrier semaphores. Data moves between devices by JAX's collectives and lax.ppermute only.
A program may use at most 128 MiB of HBM per device.

```python
import jax
import jax.numpy as jnp
from jax import lax

SIDE = 32
PIX = 1024
CHANNELS = 3
CLASSES = 10
LAYERS = 2
SUP = 256
TGT = 256


def set_ends(entries, key, smallest, largest):
    extent = entries.shape
    place = [jax.random.randint(jax.random.fold_in(key, axis), (), 0, extent[axis]) for axis in range(len(extent))]
    entries = entries.at[tuple(place)].set(smallest)
    longest = extent.index(max(extent))
    place[longest] = (place[longest] + 1) % extent[longest]
    return entries.at[tuple(place)].set(largest)


def level_of(rng, extent, pieces, low, top_value):
    gain, own = 1.0, jax.random.fold_in(rng, 6)
    for dim, blocks in pieces:
        heights = jnp.exp(jax.random.uniform(jax.random.fold_in(own, dim), (blocks,), jnp.float32, low / len(pieces), top_value / len(pieces)))
        gain = gain * jnp.repeat(heights, extent[dim] // blocks).reshape([-1 if axis == dim else 1 for axis in range(len(extent))])
    return gain


def normal_values(rng, shape, spread, bound, cuts=(), kind=jnp.bfloat16):
    array = spread * jax.random.normal(rng, shape, jnp.float32)
    if cuts:
        array = array * level_of(rng, shape, cuts, -0.22, 0.18)
    return jnp.clip(array, -bound, bound).astype(kind)


def setup_inputs(seed: int = 0) -> dict:
    splits = jax.random.split(jax.random.key(seed), 5)
    return {
        "support": normal_values(splits[0], (SUP, CHANNELS, PIX), 1.0, 6.0, ((0, 256),), jnp.float32),
        "support_labels": set_ends(jax.random.randint(splits[1], (SUP,), 0, CLASSES), jax.random.fold_in(splits[1], 1), 0, CLASSES - 1).astype(jnp.int32),
        "targets": normal_values(splits[2], (TGT, CHANNELS, PIX), 1.0, 6.0, ((0, 8),), jnp.float32),
        "target_labels": set_ends(jax.random.randint(splits[3], (TGT,), 0, CLASSES), jax.random.fold_in(splits[3], 1), 0, CLASSES - 1).astype(jnp.int32),
    }


def stencil(maps):
    column = jnp.arange(maps.shape[-1], dtype=jnp.int32) % SIDE
    zero_col = jnp.zeros(maps.shape[:-1] + (1,), maps.dtype)
    from_left = jnp.concatenate([zero_col, maps[..., :-1]], axis=-1) * (column != 0).astype(maps.dtype)
    from_right = jnp.concatenate([maps[..., 1:], zero_col], axis=-1) * (column != SIDE - 1).astype(maps.dtype)
    across = maps + from_left + from_right
    zero_row = jnp.zeros(maps.shape[:-1] + (SIDE,), maps.dtype)
    from_above = jnp.concatenate([zero_row, across[..., :-SIDE]], axis=-1)
    from_below = jnp.concatenate([across[..., SIDE:], zero_row], axis=-1)
    return across + from_above + from_below

def arc_maps(sigmas, var_left, var_right):
    scales = jnp.sqrt(var_left * var_right)
    cosine = jnp.clip(sigmas / scales, -0.9999, 0.9999)
    remain = jnp.pi - jnp.arccos(cosine)
    expect = scales * (jnp.sqrt(1.0 - cosine * cosine) + remain * cosine) / (2.0 * jnp.pi)
    slopes = remain / (2.0 * jnp.pi)
    return (expect, slopes)

def self_vars(images):
    first = 2.0 / 27.0 * stencil(lax.optimization_barrier(jnp.sum(images * images, axis=1))) + 0.1
    result = [first]
    for depth_index in range(1, LAYERS):
        result.append(2.0 / 9.0 * stencil(0.5 * result[-1]) + 0.1)
    return result

def ntk_block(left, right):
    vars_left = self_vars(left)
    vars_right = self_vars(right)
    crossed = lax.optimization_barrier(jnp.sum(left[:, None] * right[None], axis=2))
    sigmas = 2.0 / 27.0 * stencil(crossed) + 0.1
    thetas = sigmas
    for depth_index in range(1, LAYERS):
        expect, slopes = arc_maps(sigmas, vars_left[depth_index - 1][:, None], vars_right[depth_index - 1][None])
        sigmas = 2.0 / 9.0 * stencil(expect) + 0.1
        thetas = sigmas + 2.0 / 9.0 * stencil(slopes * thetas)
    expect, slopes = arc_maps(sigmas, vars_left[-1][:, None], vars_right[-1][None])
    return 2.0 / left.shape[-1] * lax.optimization_barrier(jnp.sum(expect + slopes * thetas, axis=-1))

def kernel_rows(left, right):
    stacked = left.reshape(left.shape[0] // 16, 16, left.shape[1], left.shape[2])
    blocks = lax.map(lambda piece: ntk_block(piece, right), stacked)
    return blocks.reshape(left.shape[0], right.shape[0])

def one_hot(labels):
    return (labels[:, None] == jnp.arange(CLASSES, dtype=jnp.int32)[None]).astype(jnp.float32) - 0.1

def reference(support, support_labels, targets, target_labels):
    ys_hot = one_hot(support_labels)
    yt_hot = one_hot(target_labels)
    kernel_ss = kernel_rows(support, support)
    kernel_ts = kernel_rows(targets, support)

    def loss_of(kss, kts):
        ridge = 0.1 * jnp.trace(kss) / kss.shape[0]
        coeffs = jnp.linalg.solve(kss + ridge * jnp.eye(kss.shape[0], dtype=kss.dtype), ys_hot)
        residual = jnp.dot(kts, coeffs, precision=lax.Precision.HIGHEST) - yt_hot
        return 0.5 * jnp.sum(residual * residual)
    objective, pullback = jax.vjp(loss_of, kernel_ss, kernel_ts)
    grad_ss, grad_ts = pullback(jnp.ones_like(objective))

    def support_step(step_index, accum):
        begin = (step_index * 16).astype(jnp.int32)
        piece = lax.dynamic_slice_in_dim(support, begin, 16, 0)
        cotangent = lax.dynamic_slice_in_dim(grad_ss, begin, 16, 0)
        _, back_fn = jax.vjp(ntk_block, piece, support)
        d_piece, d_all = back_fn(cotangent)
        accum = accum + d_all
        return lax.dynamic_update_slice_in_dim(accum, lax.dynamic_slice_in_dim(accum, begin, 16, 0) + d_piece, begin, 0)

    def target_step(step_index, accum):
        begin = (step_index * 16).astype(jnp.int32)
        piece = lax.dynamic_slice_in_dim(targets, begin, 16, 0)
        cotangent = lax.dynamic_slice_in_dim(grad_ts, begin, 16, 0)
        _, back_fn = jax.vjp(lambda images: ntk_block(piece, images), support)
        return accum + back_fn(cotangent)[0]
    accum = jnp.zeros_like(support)
    accum = lax.fori_loop(0, support.shape[0] // 16, support_step, accum)
    accum = lax.fori_loop(0, targets.shape[0] // 16, target_step, accum)
    return (accum, objective)
```

```python
import functools
import math

import jax
import jax.numpy as jnp
from jax import lax
from jax.experimental import pallas as pl
from jax.experimental.pallas import tpu as pltpu
from jax.sharding import PartitionSpec as P

SIDE = 32
CLASSES = 10
BOTH = ("tgt", "sup")
LANES = 128
FOUR = 4
ALPHA1 = (2.0 / 9.0) / (2.0 * math.pi)
ALPHA2 = 1.0 / (2.0 * math.pi)
FIRST = 2.0 / 27.0
SECOND = 2.0 / 9.0
ACOS = (
    1.5707963050,
    -0.2145988016,
    0.0889789874,
    -0.0501743046,
    0.0308918810,
    -0.0170881256,
    0.0066700901,
    -0.0012624911,
)
VMEM_LIMIT = 56 * 1024 * 1024
HIGHEST = lax.Precision.HIGHEST


def lane_index(shape):
    return lax.broadcasted_iota(jnp.int32, shape, len(shape) - 1)


def across(x, keep_left, keep_right):
    axis = x.ndim - 1
    return x + pltpu.roll(x, 1, axis) * keep_left + pltpu.roll(x, LANES - 1, axis) * keep_right


def edge_masks(shape):
    column = lane_index(shape) % SIDE
    return (column != 0).astype(jnp.float32), (column != SIDE - 1).astype(jnp.float32)


def swap_blocks(x0, x1, x2, x3):
    lane = lane_index(x0.shape)
    low = lane < 64
    even = (lane // SIDE) % 2 == 0
    axis = x0.ndim - 1
    a0 = jnp.where(low, x0, pltpu.roll(x2, 64, axis))
    a2 = jnp.where(low, pltpu.roll(x0, 64, axis), x2)
    a1 = jnp.where(low, x1, pltpu.roll(x3, 64, axis))
    a3 = jnp.where(low, pltpu.roll(x1, 64, axis), x3)
    y0 = jnp.where(even, a0, pltpu.roll(a1, 32, axis))
    y1 = jnp.where(even, pltpu.roll(a0, 96, axis), a1)
    y2 = jnp.where(even, a2, pltpu.roll(a3, 32, axis))
    y3 = jnp.where(even, pltpu.roll(a2, 96, axis), a3)
    return y0, y1, y2, y3


def spread_blocks(y):
    lane = lane_index(y.shape)
    low = lane < 64
    even = (lane // SIDE) % 2 == 0
    axis = y.ndim - 1
    turned = pltpu.roll(y, 64, axis)
    first = jnp.where(low, y, turned)
    last = jnp.where(low, turned, y)
    first_turned = pltpu.roll(first, 32, axis)
    last_turned = pltpu.roll(last, 32, axis)
    return (
        jnp.where(even, first, first_turned),
        jnp.where(even, first_turned, first),
        jnp.where(even, last, last_turned),
        jnp.where(even, last_turned, last),
    )


def column_kernel(images_ref, pack_ref):
    keep_left, keep_right = edge_masks((8, LANES))
    for c in range(3):
        for s in range(8):
            y = images_ref[pl.ds(c * 8 + s, 8, stride=32), :]
            for k, z in enumerate(spread_blocks(y)):
                pack_ref[c, 4 * s + k] = z
    sums = []
    for r in range(SIDE):
        b0, b1, b2 = pack_ref[0, r], pack_ref[1, r], pack_ref[2, r]
        sums.append(across(b0 * b0 + b1 * b1 + b2 * b2, keep_left, keep_right))
    variances = []
    for r in range(SIDE):
        total = sums[r]
        if r > 0:
            total = total + sums[r - 1]
        if r < SIDE - 1:
            total = total + sums[r + 1]
        q = FIRST * total + 0.1
        inverse = lax.rsqrt(q)
        pack_ref[3, r] = inverse
        pack_ref[4, r] = q * inverse
        variances.append(across(q, keep_left, keep_right))
    for r in range(SIDE):
        total = variances[r]
        if r > 0:
            total = total + variances[r - 1]
        if r < SIDE - 1:
            total = total + variances[r + 1]
        q = (0.5 * SECOND) * total + 0.1
        inverse = lax.rsqrt(q)
        pack_ref[5, r] = inverse
        pack_ref[6, r] = q * inverse


def arc(sigma, inverse, scale, alpha, bump):
    raw = sigma * inverse
    if bump is not None:
        raw = raw + bump
    cosine = jnp.minimum(jnp.maximum(raw, -0.9999), 0.9999)
    inside = cosine == raw
    size = jnp.abs(cosine)
    below = 1.0 - size
    poly = jnp.float32(alpha * ACOS[-1])
    for coefficient in ACOS[-2::-1]:
        poly = poly * size + jnp.float32(alpha * coefficient)
    angle = (below * lax.rsqrt(below)) * poly
    slope = jnp.where(cosine >= 0.0, jnp.float32(alpha * math.pi) - angle, angle)
    rest = 1.0 - cosine * cosine
    root = alpha * lax.rsqrt(rest)
    value = scale * (rest * root + slope * cosine)
    return value, slope, root * inverse, inside


def maps_kernel(
    place_ref, images_ref, pack_ref, entries_ref, units_ref, planes_ref, rows_ref, *, diagonal
):
    group = pl.program_id(0)
    keep_left, keep_right = edge_masks((8, LANES))
    sublane = lax.broadcasted_iota(jnp.int32, (8, LANES), 0)

    for c in range(3):
        planes = swap_blocks(*[images_ref[i, c] for i in range(FOUR)])
        for k in range(FOUR):
            rows_ref[c, k] = planes[k]

    def down(planes):
        result = []
        for k in range(FOUR):
            above = planes[k - 1]
            if k == 0:
                above = jnp.where(sublane == 0, 0.0, pltpu.roll(planes[FOUR - 1], 1, 0))
            under = planes[(k + 1) % FOUR]
            if k == FOUR - 1:
                under = jnp.where(sublane == 7, 0.0, pltpu.roll(planes[0], 7, 0))
            result.append(planes[k] + above + under)
        return result

    squares = [
        across(sum(rows_ref[c, k] * rows_ref[c, k] for c in range(3)), keep_left, keep_right)
        for k in range(FOUR)
    ]
    first = [FIRST * t + 0.1 for t in down(squares)]
    second = [
        (0.5 * SECOND) * t + 0.1 for t in down([across(q, keep_left, keep_right) for q in first])
    ]
    for k in range(FOUR):
        inverse1 = lax.rsqrt(first[k])
        inverse2 = lax.rsqrt(second[k])
        rows_ref[3, k] = inverse1
        rows_ref[4, k] = first[k] * inverse1
        rows_ref[5, k] = inverse2
        rows_ref[6, k] = second[k] * inverse2
    for c in range(3):
        for k in range(FOUR):
            plane = FIRST * rows_ref[c, k]
            rows_ref[c, k] = plane
            planes_ref[0, c, k] = plane

    def row(c, r):
        return jnp.broadcast_to(rows_ref[c, r % FOUR, pl.ds(r // FOUR, 1), :], (8, LANES))

    bump = None
    if diagonal:
        own_row = place_ref[1]
        image = group * FOUR + lane_index((8, LANES)) // SIDE
        own = jnp.logical_and(image == own_row, sublane == place_ref[0])
        bump = own.astype(jnp.float32)

    def vertical(window, r):
        total = window[r]
        if r > 0:
            total = total + window[r - 1]
        if r < SIDE - 1:
            total = total + window[r + 1]
        return total

    cross, value_sum, slope_sum, dsig_sum, ds2_sum, dtheta_sum = {}, {}, {}, {}, {}, {}
    kept = {}
    total = jnp.zeros((8, LANES), jnp.float32)
    for step in range(SIDE + 4):
        r = step
        if r < SIDE:
            x = row(0, r) * pack_ref[0, r] + row(1, r) * pack_ref[1, r] + row(2, r) * pack_ref[2, r]
            cross[r] = across(x, keep_left, keep_right)
        r = step - 1
        if 0 <= r < SIDE:
            sigma = vertical(cross, r) + 0.1
            inverse = row(3, r) * pack_ref[3, r]
            scale = row(4, r) * pack_ref[4, r]
            value, slope, weight, inside = arc(sigma, inverse, scale, ALPHA1, None)
            value_sum[r] = across(value, keep_left, keep_right)
            slope_sum[r] = across(slope * sigma, keep_left, keep_right)
            kept[r] = (
                sigma,
                value,
                slope,
                jnp.where(inside, slope, 0.0),
                jnp.where(inside, sigma * weight, 0.0),
            )
        r = step - 2
        if 0 <= r < SIDE:
            sigma = vertical(value_sum, r) + 0.1
            theta = sigma + vertical(slope_sum, r)
            inverse = row(5, r) * pack_ref[5, r]
            scale = row(6, r) * pack_ref[6, r]
            value, slope, weight, inside = arc(sigma, inverse, scale, ALPHA2, bump)
            total = total + (value + slope * theta)
            dsigma = jnp.where(inside, slope + theta * weight, 0.0)
            units_ref[0, 2, r] = value - dsigma * sigma
            ds2_sum[r] = across(slope, keep_left, keep_right)
            dsig_sum[r] = across(dsigma + slope, keep_left, keep_right)
        r = step - 3
        if 0 <= r < SIDE:
            sigma, value, slope, slope_in, weight_in = kept.pop(r)
            dvalue = vertical(dsig_sum, r)
            dproduct = vertical(ds2_sum, r)
            inner = slope_in * dvalue + dproduct * weight_in
            units_ref[0, 1, r] = value * dvalue - inner * sigma
            dtheta_sum[r] = across(inner + dproduct * slope, keep_left, keep_right)
        r = step - 4
        if 0 <= r < SIDE:
            units_ref[0, 0, r] = vertical(dtheta_sum, r)

    lane = lane_index((LANES, LANES))
    pick = lane == group * FOUR + lax.broadcasted_iota(jnp.int32, (LANES, LANES), 0) // SIDE
    part = jnp.dot(
        total * (2.0 / 1024.0),
        pick.astype(jnp.float32),
        precision=HIGHEST,
        preferred_element_type=jnp.float32,
    )

    @pl.when(group == 0)
    def _():
        entries_ref[...] = part

    @pl.when(group > 0)
    def _():
        entries_ref[...] += part


def halves(x):
    high = x.astype(jnp.bfloat16)
    return high, (x - high.astype(jnp.float32)).astype(jnp.bfloat16)


def product3(a, b):
    (ah, al), (bh, bl) = a, b
    dot = functools.partial(jnp.dot, preferred_element_type=jnp.float32)
    return dot(ah, bh) + (dot(ah, bl) + dot(al, bh))


def exact(a, b):
    return jnp.dot(a, b, precision=HIGHEST, preferred_element_type=jnp.float32)


def exact_nt(a, b):
    return lax.dot_general(
        a,
        b,
        (((1,), (1,)), ((), ())),
        precision=HIGHEST,
        preferred_element_type=jnp.float32,
    )


def solve_kernel(
    place_ref,
    received_ref,
    support_labels_ref,
    target_labels_ref,
    pack_ref,
    units_t_hbm,
    units_s_hbm,
    planes_t_ref,
    planes_s_ref,
    grad_ref,
    objective_ref,
    units_ref,
    kernel_ref,
    cross_ref,
    inverse_ref,
    weights_ref,
    grads_ref,
    sem,
):
    copies = [
        pltpu.make_async_copy(units_t_hbm, units_ref.at[pl.ds(0, 8)], sem.at[0]),
        pltpu.make_async_copy(units_s_hbm, units_ref.at[pl.ds(8, 8)], sem.at[1]),
    ]
    for copy in copies:
        copy.start()

    for which, out_ref in ((0, kernel_ref), (1, cross_ref)):
        for q in range(2):
            for h in range(2):
                blocks = []
                for i in range(FOUR):
                    start = (4 * h + i) * 32 * 4 + 2 * which + q
                    blocks.append(received_ref[pl.ds(start, 32, stride=4), :])
                for j, y in enumerate(swap_blocks(*blocks)):
                    out_ref[pl.ds((4 * q + j) * 32, 32), pl.ds(h * LANES, LANES)] = y

    count = 256
    matrix = kernel_ref[...]
    row_id = lax.broadcasted_iota(jnp.int32, (count, count), 0)
    col_id = lax.broadcasted_iota(jnp.int32, (count, count), 1)
    eye = row_id == col_id
    trace = jnp.sum(jnp.where(eye, matrix, 0.0))
    ridge = 0.1 * trace / count
    matrix = matrix + jnp.where(eye, ridge, 0.0)
    kernel_ref[...] = matrix
    bound = jnp.max(jnp.sum(jnp.abs(matrix), axis=0, keepdims=True))
    spread = (bound - ridge) / (bound + ridge)
    start = 2.0 / (bound + ridge)
    square = spread * spread
    gain = 2.0 / (2.0 - square)
    inverse_ref[...] = (gain * start) * (jnp.where(eye, 2.0, 0.0) - start * matrix)
    matrix_halves = halves(matrix)

    def refine(delta):
        square = delta * delta
        gain = 2.0 / (2.0 - square)
        x = inverse_ref[...]
        x_halves = halves(x)
        error = jnp.where(eye, 1.0, 0.0) - product3(matrix_halves, x_halves)
        inverse_ref[...] = gain * (x + product3(x_halves, halves(error)))
        return square / (2.0 - square)

    lax.while_loop(lambda delta: delta > 3e-3, refine, square / (2.0 - square))
    x = inverse_ref[...]
    inverse = x + exact(x, jnp.where(eye, 1.0, 0.0) - exact(matrix, x))

    def solve(right):
        guess = exact(right, inverse)
        for _ in range(2):
            guess = guess + exact(right - exact(guess, matrix), inverse)
        return guess

    class_id = lax.broadcasted_iota(jnp.int32, (16, count), 0)

    def one_hot(labels):
        hot = (class_id == labels).astype(jnp.float32) - 0.1
        return jnp.where(class_id < CLASSES, hot, 0.0)

    coeffs = solve(one_hot(support_labels_ref[...]))
    cross = cross_ref[...]
    residual = exact(coeffs, cross) - one_hot(target_labels_ref[...])
    objective_ref[...] = jnp.full((8, LANES), 0.5 * jnp.sum(residual * residual), jnp.float32)
    adjoint = solve(exact_nt(residual, cross))
    trace_grad = -jnp.sum(adjoint * coeffs)

    mine_t, mine_s = place_ref[0], place_ref[1]
    ids = lax.broadcasted_iota(jnp.int32, (8, count), 1)
    mine = lax.broadcasted_iota(jnp.int32, (8, count), 0) * 32 + mine_s
    pick_columns = (ids == mine).astype(jnp.float32)
    coeffs_col = exact_nt(pick_columns, coeffs)
    adjoint_col = exact_nt(pick_columns, adjoint)
    pick_rows = (
        lax.broadcasted_iota(jnp.int32, (count, LANES), 0)
        == lax.broadcasted_iota(jnp.int32, (count, LANES), 1) + mine_t * 32
    ).astype(jnp.float32)
    coeffs_row = exact(coeffs, pick_rows)
    adjoint_row = exact(adjoint, pick_rows)
    residual_row = exact(residual, pick_rows)
    pair_ts = exact(coeffs_col, residual_row)
    pair_ss = -(exact(coeffs_col, adjoint_row) + exact(adjoint_col, coeffs_row))
    sub8 = lax.broadcasted_iota(jnp.int32, (8, LANES), 0)
    lane8 = lane_index((8, LANES))
    own = jnp.logical_and(sub8 == mine_t, lane8 == mine_s)
    pair_ss = pair_ss + jnp.where(own, (0.2 / count) * trace_grad, 0.0)
    widen = (
        lax.broadcasted_iota(jnp.int32, (LANES, 1024), 0)
        == lax.broadcasted_iota(jnp.int32, (LANES, 1024), 1) // SIDE
    ).astype(jnp.float32)
    for which, pair in ((0, pair_ts), (1, pair_ss)):
        wide = exact(pair * (2.0 / 1024.0), widen)
        for g in range(8):
            weights_ref[8 * which + g] = wide[:, g * LANES : (g + 1) * LANES]

    for copy in copies:
        copy.wait()

    weights = [weights_ref[g] for g in range(16)]

    def gather_row(s, carry):
        for k in range(FOUR):
            r = s * FOUR + k
            sums = [None] * 5
            for g in range(16):
                planes_ref = planes_t_ref if g < 8 else planes_s_ref
                weight = weights[g]
                dx = weight * units_ref[g, 0, r]
                terms = [
                    dx * jnp.broadcast_to(planes_ref[g % 8, c, k, pl.ds(s, 1), :], (8, LANES))
                    for c in range(3)
                ]
                terms.append(weight * units_ref[g, 1, r])
                terms.append(weight * units_ref[g, 2, r])
                sums = [t if a is None else a + t for a, t in zip(sums, terms)]
            for n, total in enumerate(sums):
                total = total + pltpu.roll(total, 64, 1)
                grads_ref[n, r] = total + pltpu.roll(total, 32, 1)
        return carry

    lax.fori_loop(0, 8, gather_row, 0)

    keep_left, keep_right = edge_masks((8, LANES))

    def vertical(window, r):
        total = window[r]
        if r > 0:
            total = total + window[r - 1]
        if r < SIDE - 1:
            total = total + window[r + 1]
        return total

    second, first = {}, {}
    for r in range(SIDE):
        inverse2 = pack_ref[5, r]
        second[r] = across(0.5 * inverse2 * inverse2 * grads_ref[4, r], keep_left, keep_right)
    for r in range(SIDE):
        inverse1 = pack_ref[3, r]
        dq1 = 0.5 * inverse1 * inverse1 * grads_ref[3, r] + (0.5 * SECOND) * vertical(second, r)
        first[r] = across(dq1, keep_left, keep_right)
    lane = lane8 // SIDE
    for s in range(8):
        scales = [(2.0 * FIRST) * vertical(first, 4 * s + k) for k in range(FOUR)]
        for c in range(3):
            full = [
                grads_ref[c, 4 * s + k] + pack_ref[c, 4 * s + k] * scales[k] for k in range(FOUR)
            ]
            merged = jnp.where(
                lane < 2,
                jnp.where(lane == 0, full[0], full[1]),
                jnp.where(lane == 2, full[2], full[3]),
            )
            grad_ref[pl.ds(c * 8 + s, 8, stride=24), :] = merged


def params():
    return pltpu.CompilerParams(vmem_limit_bytes=VMEM_LIMIT)


def f32(*shape):
    return jax.ShapeDtypeStruct(shape, jnp.float32)


def column_pack(images):
    return pl.pallas_call(
        column_kernel,
        out_shape=f32(7, SIDE, 8, LANES),
        compiler_params=params(),
    )(images)


def pair_maps(place, images, pack, diagonal):
    groups = images.shape[0] // FOUR
    return pl.pallas_call(
        functools.partial(maps_kernel, diagonal=diagonal),
        grid=(groups,),
        in_specs=[
            pl.BlockSpec(memory_space=pltpu.SMEM),
            pl.BlockSpec((FOUR, 3, 8, LANES), lambda g: (g, 0, 0, 0)),
            pl.BlockSpec((7, SIDE, 8, LANES), lambda g: (0, 0, 0, 0)),
        ],
        out_specs=[
            pl.BlockSpec((8, LANES), lambda g: (0, 0)),
            pl.BlockSpec((1, 3, SIDE, 8, LANES), lambda g: (g, 0, 0, 0, 0)),
            pl.BlockSpec((1, 3, FOUR, 8, LANES), lambda g: (g, 0, 0, 0, 0)),
        ],
        out_shape=[
            f32(8, LANES),
            f32(groups, 3, SIDE, 8, LANES),
            f32(groups, 3, FOUR, 8, LANES),
        ],
        scratch_shapes=[pltpu.VMEM((7, FOUR, 8, LANES), jnp.float32)],
        compiler_params=params(),
        cost_estimate=pl.CostEstimate(
            flops=groups * 32 * 1024 * 140, bytes_accessed=4 << 20, transcendentals=0
        ),
    )(place, images, pack)


def solve_and_grad(place, received, support_labels, target_labels, pack, units, planes):
    vmem = pl.BlockSpec(memory_space=pltpu.VMEM)
    return pl.pallas_call(
        solve_kernel,
        in_specs=[pl.BlockSpec(memory_space=pltpu.SMEM)]
        + [vmem] * 4
        + [pl.BlockSpec(memory_space=pl.ANY)] * 2
        + [vmem] * 2,
        out_specs=[vmem, vmem],
        out_shape=[f32(192, LANES), f32(8, LANES)],
        scratch_shapes=[
            pltpu.VMEM((16, 3, SIDE, 8, LANES), jnp.float32),
            pltpu.VMEM((256, 256), jnp.float32),
            pltpu.VMEM((256, 256), jnp.float32),
            pltpu.VMEM((256, 256), jnp.float32),
            pltpu.VMEM((16, 8, LANES), jnp.float32),
            pltpu.VMEM((5, SIDE, 8, LANES), jnp.float32),
            pltpu.SemaphoreType.DMA((2,)),
        ],
        compiler_params=params(),
    )(place, received, support_labels, target_labels, pack, *units, *planes)


def on_device(support, support_labels, targets, target_labels):
    tgt_id, sup_id = lax.axis_index("tgt"), lax.axis_index("sup")
    place = jnp.stack([tgt_id, sup_id]).astype(jnp.int32)
    image = support.reshape(24, LANES)
    label_row = jnp.zeros((8, LANES), jnp.float32)
    label_row = label_row.at[0, :32].set(target_labels.astype(jnp.float32))
    message = jnp.concatenate([image, label_row], axis=0)
    columns = lax.all_to_all(
        jnp.broadcast_to(message, (8, 32, LANES)), "tgt", 0, 0, tiled=True
    )
    rows = lax.all_to_all(
        jnp.broadcast_to(image.reshape(3, 8, LANES), (32, 3, 8, LANES)), "sup", 0, 0, tiled=True
    )
    all_labels = columns[:, 24, :32].reshape(1, 256).astype(jnp.int32)
    pack = column_pack(columns.reshape(256, LANES))
    entries_t, units_t, planes_t = pair_maps(
        place, targets.reshape(32, 3, 8, LANES), pack, False
    )
    entries_s, units_s, planes_s = pair_maps(place, rows, pack, True)
    payload = jnp.stack([entries_s[:, :32].reshape(2, LANES), entries_t[:, :32].reshape(2, LANES)])
    received = lax.all_to_all(
        jnp.broadcast_to(payload.reshape(4, LANES), (256, 4, LANES)), BOTH, 0, 0, tiled=True
    )
    partial, objective = solve_and_grad(
        place,
        received.reshape(1024, LANES),
        support_labels.reshape(1, 256),
        all_labels,
        pack,
        (units_t, units_s),
        (planes_t, planes_s),
    )
    pieces = lax.all_to_all(partial.reshape(8, 3, 8, LANES), "tgt", 0, 0, tiled=True)
    return jnp.sum(pieces, axis=0).reshape(1, 3, 1024), objective[0, 0]


def solution(mesh):
    placed = (P(BOTH, None, None), P(), P("tgt", None, None), P("tgt"))
    return jax.shard_map(
        on_device,
        mesh=mesh,
        in_specs=placed,
        out_specs=(P(BOTH, None, None), P()),
        check_vma=False,
    )
```

```python
import functools
import math

import jax
import jax.numpy as jnp
from jax import lax
from jax.experimental import pallas as pl
from jax.experimental.pallas import tpu as pltpu
from jax.sharding import PartitionSpec as P

SIDE = 32
CLASSES = 10
BOTH = ("tgt", "sup")
LANES = 128
FOUR = 4
ALPHA1 = (2.0 / 9.0) / (2.0 * math.pi)
ALPHA2 = 1.0 / (2.0 * math.pi)
FIRST = 2.0 / 27.0
SECOND = 2.0 / 9.0
ACOS = (
    1.570796238860342,
    -0.21459108884050843,
    0.08883588680709523,
    -0.04919743925456755,
    0.027762915193263623,
    -0.01200339464235187,
    0.002611719889929782,
)
VMEM_LIMIT = 56 * 1024 * 1024
HIGHEST = lax.Precision.HIGHEST


def lane_index(shape):
    return lax.broadcasted_iota(jnp.int32, shape, len(shape) - 1)


def across(x, keep_left, keep_right):
    axis = x.ndim - 1
    return x + pltpu.roll(x, 1, axis) * keep_left + pltpu.roll(x, LANES - 1, axis) * keep_right


def edge_masks(shape):
    column = lane_index(shape) % SIDE
    return (column != 0).astype(jnp.float32), (column != SIDE - 1).astype(jnp.float32)


def swap_blocks(x0, x1, x2, x3):
    lane = lane_index(x0.shape)
    low = lane < 64
    even = (lane // SIDE) % 2 == 0
    axis = x0.ndim - 1
    a0 = jnp.where(low, x0, pltpu.roll(x2, 64, axis))
    a2 = jnp.where(low, pltpu.roll(x0, 64, axis), x2)
    a1 = jnp.where(low, x1, pltpu.roll(x3, 64, axis))
    a3 = jnp.where(low, pltpu.roll(x1, 64, axis), x3)
    y0 = jnp.where(even, a0, pltpu.roll(a1, 32, axis))
    y1 = jnp.where(even, pltpu.roll(a0, 96, axis), a1)
    y2 = jnp.where(even, a2, pltpu.roll(a3, 32, axis))
    y3 = jnp.where(even, pltpu.roll(a2, 96, axis), a3)
    return y0, y1, y2, y3


def spread_blocks(y):
    lane = lane_index(y.shape)
    low = lane < 64
    even = (lane // SIDE) % 2 == 0
    axis = y.ndim - 1
    turned = pltpu.roll(y, 64, axis)
    first = jnp.where(low, y, turned)
    last = jnp.where(low, turned, y)
    first_turned = pltpu.roll(first, 32, axis)
    last_turned = pltpu.roll(last, 32, axis)
    return (
        jnp.where(even, first, first_turned),
        jnp.where(even, first_turned, first),
        jnp.where(even, last, last_turned),
        jnp.where(even, last_turned, last),
    )


def message_kernel(image_ref, labels_ref, column_ref, row_ref):
    image = image_ref[...]
    hot = labels_ref[...].astype(jnp.float32)
    labels = jnp.broadcast_to(jnp.concatenate([hot] * FOUR, axis=1), (8, LANES))
    for d in range(8):
        column_ref[d, pl.ds(0, 24), :] = image
        column_ref[d, pl.ds(24, 8), :] = labels
    for d in range(row_ref.shape[0]):
        row_ref[d] = image


def column_maps(images_ref, pack_ref):
    keep_left, keep_right = edge_masks((8, LANES))
    for c in range(3):
        for s in range(8):
            y = images_ref[pl.ds(c * 8 + s, 8, stride=32), :]
            for k, z in enumerate(spread_blocks(y)):
                pack_ref[c, 4 * s + k] = z
    sums, variances = {}, {}
    for r in range(SIDE):
        b0, b1, b2 = pack_ref[0, r], pack_ref[1, r], pack_ref[2, r]
        sums[r] = across(b0 * b0 + b1 * b1 + b2 * b2, keep_left, keep_right)
    for r in range(SIDE):
        q = FIRST * vertical(sums, r) + 0.1
        inverse = lax.rsqrt(q)
        pack_ref[3, r] = inverse
        pack_ref[4, r] = q * inverse
        variances[r] = across(q, keep_left, keep_right)
    for r in range(SIDE):
        q = (0.5 * SECOND) * vertical(variances, r) + 0.1
        inverse = lax.rsqrt(q)
        pack_ref[5, r] = inverse
        pack_ref[6, r] = q * inverse


def row_maps(images, rows_ref):
    keep_left, keep_right = edge_masks((8, LANES))
    sublane = lax.broadcasted_iota(jnp.int32, (8, LANES), 0)

    def down(planes):
        above = jnp.where(sublane == 0, 0.0, pltpu.roll(planes[FOUR - 1], 1, 0))
        under = jnp.where(sublane == 7, 0.0, pltpu.roll(planes[0], 7, 0))
        line = [above, *planes, under]
        return [line[k] + line[k + 1] + line[k + 2] for k in range(FOUR)]

    squares = [0.0] * FOUR
    for c in range(3):
        planes = swap_blocks(*[images(i, c) for i in range(FOUR)])
        for k in range(FOUR):
            rows_ref[c, k] = FIRST * planes[k]
            squares[k] = squares[k] + planes[k] * planes[k]
    squares = [across(x, keep_left, keep_right) for x in squares]
    first = [FIRST * t + 0.1 for t in down(squares)]
    second = [
        (0.5 * SECOND) * t + 0.1 for t in down([across(q, keep_left, keep_right) for q in first])
    ]
    for k in range(FOUR):
        for n, q in ((3, first[k]), (5, second[k])):
            inverse = lax.rsqrt(q)
            rows_ref[n, k] = inverse
            rows_ref[n + 1, k] = q * inverse


def vertical(window, r):
    total = window[r]
    if r > 0:
        total = total + window[r - 1]
    if r < SIDE - 1:
        total = total + window[r + 1]
    return total


def vertical_pair(window, r, offset=None):
    both = window[r] + window[r + 1]
    if offset is not None:
        both = both + offset
    upper = both + window[r - 1] if r > 0 else both
    lower = both + window[r + 2] if r + 2 < SIDE else both
    return upper, lower


def arc(sigma, inverse, scale, alpha, bump):
    raw = sigma * inverse
    if bump is not None:
        raw = raw + bump
    cosine = jnp.clip(raw, -0.9999, 0.9999)
    inside = cosine == raw
    size = jnp.abs(cosine)
    below = 1.0 - size
    poly = jnp.float32(alpha * ACOS[-1])
    for coefficient in ACOS[-2::-1]:
        poly = poly * size + jnp.float32(alpha * coefficient)
    angle = (below * lax.rsqrt(below)) * poly
    slope = jnp.where(cosine >= 0.0, jnp.float32(alpha * math.pi) - angle, angle)
    rest = 1.0 - cosine * cosine
    root = alpha * lax.rsqrt(rest)
    value = scale * (rest * root + slope * cosine)
    return value, slope, root * inverse, inside


def group_maps(rows_ref, pack_ref, units_ref, bump):
    keep_left, keep_right = edge_masks((8, LANES))

    def row(c, r):
        return jnp.broadcast_to(rows_ref[c, r % FOUR, pl.ds(r // FOUR, 1), :], (8, LANES))

    cross, value_sum, slope_sum, dsig_sum, ds2_sum, dtheta_sum = {}, {}, {}, {}, {}, {}
    kept = {}
    total = jnp.zeros((8, LANES), jnp.float32)
    for step in range(0, SIDE + 10, 2):
        for r in (step, step + 1):
            if r < SIDE:
                x = sum(row(c, r) * pack_ref[c, r] for c in range(3))
                cross[r] = across(x, keep_left, keep_right)
        base = step - 2
        if 0 <= base < SIDE:
            for r, sigma in zip((base, base + 1), vertical_pair(cross, base, 0.1)):
                inverse = row(3, r) * pack_ref[3, r]
                scale = row(4, r) * pack_ref[4, r]
                value, slope, weight, inside = arc(sigma, inverse, scale, ALPHA1, None)
                value_sum[r] = across(value, keep_left, keep_right)
                slope_sum[r] = across(slope * sigma, keep_left, keep_right)
                if units_ref is not None:
                    kept[r] = (
                        sigma,
                        value,
                        slope,
                        jnp.where(inside, slope, 0.0),
                        jnp.where(inside, sigma * weight, 0.0),
                    )
        base = step - 4
        if 0 <= base < SIDE:
            for r, sigma, more in zip(
                (base, base + 1),
                vertical_pair(value_sum, base, 0.1),
                vertical_pair(slope_sum, base),
            ):
                theta = sigma + more
                inverse = row(5, r) * pack_ref[5, r]
                scale = row(6, r) * pack_ref[6, r]
                value, slope, weight, inside = arc(sigma, inverse, scale, ALPHA2, bump)
                total = total + (value + slope * theta)
                if units_ref is not None:
                    dsigma = jnp.where(inside, slope + theta * weight, 0.0)
                    units_ref[2, r] = value - dsigma * sigma
                    ds2_sum[r] = across(slope, keep_left, keep_right)
                    dsig_sum[r] = across(dsigma + slope, keep_left, keep_right)
        if units_ref is None:
            continue
        base = step - 6
        if 0 <= base < SIDE:
            for r, dvalue, dproduct in zip(
                (base, base + 1), vertical_pair(dsig_sum, base), vertical_pair(ds2_sum, base)
            ):
                sigma, value, slope, slope_in, weight_in = kept.pop(r)
                inner = slope_in * dvalue + dproduct * weight_in
                units_ref[1, r] = value * dvalue - inner * sigma
                dtheta_sum[r] = across(inner + dproduct * slope, keep_left, keep_right)
        base = step - 8
        if 0 <= base < SIDE:
            for r, unit in zip((base, base + 1), vertical_pair(dtheta_sum, base)):
                units_ref[0, r] = unit
    return total


def sum_entries(totals_ref):
    parts = [part.astype(jnp.float32) for part in split(totals_ref[...] * (2.0 / 1024.0), 3)]
    stacked = jnp.concatenate(parts + [jnp.zeros((8, 1024), jnp.float32)], axis=0)
    source = lax.broadcasted_iota(jnp.int32, (1024, LANES), 0) // SIDE
    pick = (source == lane_index((1024, LANES))).astype(jnp.bfloat16)
    sums = dot(stacked.astype(jnp.bfloat16), pick)
    return sums[:8] + (sums[8:16] + sums[16:24])


def keep_total(totals_ref, group, total):
    totals_ref[:, pl.ds(pl.multiple_of(group * LANES, LANES), LANES)] = total


def own_bump(group):
    image = group * FOUR + lane_index((8, LANES)) // SIDE
    column = lax.broadcasted_iota(jnp.int32, (8, LANES), 0)
    mine = lax.axis_index("sup") // 2
    own = jnp.logical_and(image == mine, column == lax.axis_index("tgt"))
    return own.astype(jnp.float32)


def copy_out(units_ref, units_hbm, sems, group):
    return pltpu.make_async_copy(units_ref.at[group], units_hbm.at[group], sems.at[group])


def row_kernel(images_ref, planes_ref):
    for group in range(8):

        def image(i, c, group=group):
            n = group * FOUR + i
            lines = [images_ref[c, pl.ds(n, 1), pl.ds(s * LANES, LANES)] for s in range(8)]
            return jnp.concatenate(lines, axis=0)

        row_maps(image, planes_ref.at[group])


def target_kernel(
    planes_ref, columns_ref, entries_ref, pack_ref, inverses_ref, units_hbm, units_ref, totals_ref, sems
):
    column_maps(columns_ref, pack_ref)
    block = lane_index((8, LANES)) // SIDE
    for n in range(2):
        for s in range(8):
            inverses_ref[n, s] = pick_blocks([pack_ref[3 + 2 * n, 4 * s + k] for k in range(FOUR)], block)

    def body(group, carry):
        keep_total(
            totals_ref,
            group,
            group_maps(planes_ref.at[group], pack_ref, units_ref.at[group], None),
        )
        copy_out(units_ref, units_hbm, sems, group).start()
        return carry

    lax.fori_loop(0, 8, body, 0)
    entries_ref[...] = sum_entries(totals_ref)
    for group in range(8):
        copy_out(units_ref, units_hbm, sems, group).wait()


def entries_kernel(
    own_ref, other_ref, pack_ref, entries_t_ref, payload_ref, planes_ref, totals_ref
):
    for half, images_ref in enumerate((own_ref, other_ref)):
        for group in range(FOUR):
            row_maps(
                lambda i, c: images_ref[group * FOUR + i, pl.ds(c * 8, 8), :],
                planes_ref.at[half * FOUR + group],
            )

    def body(group, carry):
        total = group_maps(planes_ref.at[group], pack_ref, None, own_bump(group))
        keep_total(totals_ref, group, total)
        return carry

    lax.fori_loop(0, 8, body, 0)
    entries = sum_entries(totals_ref)
    lane = lane_index((8, LANES))
    turned = jnp.where(lane < 16, pltpu.roll(entries, LANES - 16, 1), pltpu.roll(entries, 16, 1))
    turned = jnp.where(lane < SIDE, turned, 0.0)
    entries = jnp.where(lax.axis_index("sup") % 2 == 1, turned, entries)
    both = entries + pltpu.roll(entries_t_ref[...], SIDE, 1)
    both = both + pltpu.roll(pltpu.roll(both, 64, 1), FOUR, 0)
    for d in range(payload_ref.shape[0]):
        payload_ref[d] = both[:FOUR]


def units_kernel(planes_ref, pack_ref, units_hbm, units_ref, sems):
    def body(group, carry):
        group_maps(planes_ref.at[group], pack_ref, units_ref.at[group], own_bump(group))
        copy_out(units_ref, units_hbm, sems, group).start()
        return carry

    lax.fori_loop(0, 8, body, 0)
    for group in range(8):
        copy_out(units_ref, units_hbm, sems, group).wait()


def dot(a, b):
    return jnp.dot(a, b, preferred_element_type=jnp.float32)


def dot_nt(a, b):
    return lax.dot_general(a, b, (((1,), (1,)), ((), ())), preferred_element_type=jnp.float32)


def split(x, parts):
    result = []
    for _ in range(parts):
        result.append(x.astype(jnp.bfloat16))
        x = x - result[-1].astype(jnp.float32)
    return result


def product3(a, b):
    (ah, al), (bh, bl) = a, b
    return dot(ah, bh) + (dot(ah, bl) + dot(al, bh))


def thin_exact(a, b, product=dot):
    high, middle, low = split(a, 3)
    first = product(jnp.concatenate([high, middle, low], axis=0), b[0])
    second = product(jnp.concatenate([high, middle], axis=0), b[1])
    third = product(high, b[2])
    small = first[32:48] + second[16:32] + third
    return first[:16] + (first[16:32] + second[:16] + small)


def thin_near(a, b):
    high, middle = split(a, 2)
    first = dot(jnp.concatenate([high, middle], axis=0), b[0])
    return first[:16] + (first[16:] + dot(high, b[1]))


def pick_blocks(lines, block):
    low = jnp.where(block == 0, lines[0], lines[1])
    return jnp.where(block < 2, low, jnp.where(block == 2, lines[2], lines[3]))


def merge_blocks(lines, block):
    total = pick_blocks(lines, block)
    for d in range(1, FOUR):
        moved = pick_blocks([lines[(k - d) % FOUR] for k in range(FOUR)], block)
        total = total + pltpu.roll(moved, LANES - SIDE * d, 1)
    return total


def image_stencil(lines, masks, block):
    lines = [across(x, *masks) for x in lines]
    ups = [pltpu.roll(x, SIDE, 1) for x in lines]
    downs = [pltpu.roll(x, LANES - SIDE, 1) for x in lines]
    zero = jnp.zeros_like(lines[0])
    result = []
    for s in range(8):
        up = jnp.where(block == 0, ups[s - 1] if s else zero, ups[s])
        down = jnp.where(block == 3, downs[s + 1] if s < 7 else zero, downs[s])
        result.append(lines[s] + up + down)
    return result


def solve_kernel(
    own_hbm,
    other_hbm,
    support_labels_ref,
    columns_hbm,
    inverses_hbm,
    units_t_hbm,
    units_s_hbm,
    planes_t_hbm,
    planes_s_hbm,
    grad_ref,
    objective_ref,
    received_ref,
    columns_ref,
    inverses_ref,
    units_ref,
    planes_ref,
    kernel_ref,
    inverse_ref,
    matrix_parts,
    cross_parts,
    inverse_parts,
    weights_ref,
    grads_ref,
    sems,
):
    core = lax.axis_index("sup") % 2
    copies = [
        pltpu.make_async_copy(source, target, sems.at[n])
        for n, (source, target) in enumerate(
            [
                (own_hbm, received_ref.at[core]),
                (other_hbm, received_ref.at[1 - core]),
                (columns_hbm, columns_ref),
                (inverses_hbm, inverses_ref),
                (units_t_hbm, units_ref.at[pl.ds(0, 8)]),
                (units_s_hbm, units_ref.at[pl.ds(8, 8)]),
                (planes_t_hbm.at[:, pl.ds(0, 3)], planes_ref.at[pl.ds(0, 8)]),
                (planes_s_hbm.at[:, pl.ds(0, 3)], planes_ref.at[pl.ds(8, 8)]),
            ]
        )
    ]
    for copy in copies:
        copy.start()

    count = 256
    for copy in copies[:2]:
        copy.wait()
    for half in range(2):
        for j in range(FOUR):
            for h in range(2):
                blocks = []
                for i in range(FOUR):
                    start = (FOUR * h + i) * 16 * FOUR + j
                    blocks.append(received_ref[half, pl.ds(start, 16, stride=FOUR), :])
                for b, y in enumerate(swap_blocks(*blocks)):
                    rows = pl.ds((FOUR * (b // 2) + j) * 32 + 16 * half, 16)
                    lanes = pl.ds(h * LANES, LANES)
                    if b % 2 == 0:
                        kernel_ref[rows, lanes] = y
                    else:
                        for n, part in enumerate(split(y, 3)):
                            cross_parts[n, rows, lanes] = part

    matrix = kernel_ref[...]
    row_id = lax.broadcasted_iota(jnp.int32, (count, count), 0)
    col_id = lax.broadcasted_iota(jnp.int32, (count, count), 1)
    eye = row_id == col_id
    trace = jnp.sum(jnp.where(eye, matrix, 0.0))
    ridge = 0.1 * trace / count
    matrix = matrix + jnp.where(eye, ridge, 0.0)
    bound = jnp.max(jnp.sum(jnp.abs(matrix), axis=0, keepdims=True))
    spread = (bound - ridge) / (bound + ridge)
    start = 2.0 / (bound + ridge)
    square = spread * spread
    gain = 2.0 / (2.0 - square)
    inverse_ref[...] = (gain * start) * (jnp.where(eye, 2.0, 0.0) - start * matrix)
    for n, part in enumerate(split(matrix, 3)):
        matrix_parts[n] = part

    def improve(delta):
        square = delta * delta
        gain = 2.0 / (2.0 - square)
        x = inverse_ref[...]
        parts = split(x, 2)
        error = jnp.where(eye, 1.0, 0.0) - product3((matrix_parts[0], matrix_parts[1]), parts)
        inverse_ref[...] = gain * (x + product3(parts, split(error, 2)))
        return square / (2.0 - square)

    lax.while_loop(lambda delta: delta > 3e-3, improve, square / (2.0 - square))
    for n, part in enumerate(split(inverse_ref[...], 2)):
        inverse_parts[n] = part

    def solve(right):
        def refine(state):
            guess, _, rounds = state
            rest = right - thin_exact(guess, matrix_parts)
            step = thin_near(rest, inverse_parts)
            guess = guess + step
            return guess, jnp.sum(step * step) / jnp.sum(guess * guess), rounds + 1

        def going(state):
            return jnp.logical_and(state[1] > 1e-9, state[2] < 40)

        return lax.while_loop(going, refine, (thin_near(right, inverse_parts), 1.0, 0))[0]

    class_id = lax.broadcasted_iota(jnp.int32, (16, count), 0)

    def one_hot(labels):
        hot = (class_id == labels).astype(jnp.float32) - 0.1
        return jnp.where(class_id < CLASSES, hot, 0.0)

    coeffs = solve(one_hot(support_labels_ref[...]))
    for copy in copies[2:4]:
        copy.wait()
    lane1 = lane_index((1, LANES))
    halves = []
    for h in range(2):
        line = [columns_ref[pl.ds((FOUR * h + i) * 32 + 24, 1), :] for i in range(FOUR)]
        line = [jnp.where(lane1 // SIDE == i, x, 0.0) for i, x in enumerate(line)]
        halves.append((line[0] + line[1]) + (line[2] + line[3]))
    target_labels = jnp.concatenate(halves, axis=1).astype(jnp.int32)
    residual = thin_exact(coeffs, cross_parts) - one_hot(target_labels)
    objective_ref[...] = jnp.full((8, LANES), 0.5 * jnp.sum(residual * residual), jnp.float32)
    adjoint = solve(thin_exact(residual, cross_parts, dot_nt))
    trace_grad = -jnp.sum(adjoint * coeffs)

    mine_t = lax.axis_index("tgt")
    mine = core * 16 + lax.axis_index("sup") // 2
    coeff_parts, adjoint_parts = split(coeffs, 3), split(adjoint, 3)
    ids = lax.broadcasted_iota(jnp.int32, (16, count), 1)
    wanted = lax.broadcasted_iota(jnp.int32, (16, count), 0) * 32 + mine
    picked = dot_nt(
        (ids == wanted).astype(jnp.bfloat16), jnp.concatenate(coeff_parts + adjoint_parts, axis=0)
    ).astype(jnp.bfloat16)
    turn = lax.rem(count - 32 * mine_t, count)

    def row_parts(x):
        return split(pltpu.roll(x, turn, 1)[:, :LANES], 3)

    zero = jnp.zeros((48, LANES), jnp.bfloat16)
    pairs = 0.0
    for c, a, r in zip(row_parts(-coeffs), row_parts(-adjoint), row_parts(residual)):
        side_s = jnp.concatenate([a, a, a, c, c, c], axis=0)
        side_t = jnp.concatenate([r, r, r, zero], axis=0)
        pairs = pairs + dot(picked, jnp.concatenate([side_s, side_t], axis=1))
    sub8 = lax.broadcasted_iota(jnp.int32, (8, LANES), 0)
    lane8 = lane_index((8, LANES))
    own = jnp.logical_and(sub8 == mine_t, lane8 == mine)
    pairs_s = pairs[:8, :LANES] + jnp.where(own, (0.2 / count) * trace_grad, 0.0)
    pairs = jnp.concatenate([pairs[:8, LANES:], pairs_s], axis=0)
    pairs = jnp.where(lane_index((16, LANES)) < SIDE, pairs * (2.0 / 1024.0), 0.0)
    high, middle, low = [part.astype(jnp.float32) for part in split(pairs, 3)]
    stacked = high + pltpu.roll(middle, 32, 1) + pltpu.roll(low, 64, 1)
    widen = lax.broadcasted_iota(jnp.int32, (LANES, 1024), 0) % SIDE
    widen = widen == lax.broadcasted_iota(jnp.int32, (LANES, 1024), 1) // SIDE
    wide = dot(stacked.astype(jnp.bfloat16), widen.astype(jnp.bfloat16))
    for g in range(8):
        weights_ref[g] = wide[:8, g * LANES : (g + 1) * LANES]
        weights_ref[8 + lax.rem(g + FOUR * core, 8)] = wide[8:, g * LANES : (g + 1) * LANES]

    for copy in copies[4:]:
        copy.wait()

    block = lane8 // SIDE

    def gather_line(s, carry):
        lines = [[] for _ in range(5)]
        for k in range(FOUR):
            r = s * FOUR + k
            sums = [None] * 5
            for g in range(16):
                weight = weights_ref[g]
                dx = weight * units_ref[g, 0, r]
                terms = [
                    dx * jnp.broadcast_to(planes_ref[g, c, k, pl.ds(s, 1), :], (8, LANES))
                    for c in range(3)
                ]
                terms.append(weight * units_ref[g, 1, r])
                terms.append(weight * units_ref[g, 2, r])
                sums = [t if a is None else a + t for a, t in zip(sums, terms)]
            for n in range(5):
                lines[n].append(sums[n])
        for n in range(5):
            grads_ref[n, s] = merge_blocks(lines[n], block)
        return carry

    lax.fori_loop(0, 8, gather_line, 0, unroll=2)

    masks = edge_masks((8, LANES))
    second = [0.5 * inverses_ref[1, s] * inverses_ref[1, s] * grads_ref[4, s] for s in range(8)]
    second = image_stencil(second, masks, block)
    first = [
        0.5 * inverses_ref[0, s] * inverses_ref[0, s] * grads_ref[3, s] + (0.5 * SECOND) * second[s]
        for s in range(8)
    ]
    first = image_stencil(first, masks, block)
    for s in range(8):
        for c in range(3):
            image = columns_ref[pl.ds(c * 8 + s, 8, stride=32), :]
            grad_ref[pl.ds(c * 8 + s, 8, stride=24), :] = (
                grads_ref[c, s] + (2.0 * FIRST) * first[s] * image
            )


def f32(*shape):
    return jax.ShapeDtypeStruct(shape, jnp.float32)


HBM = pl.BlockSpec(memory_space=pl.ANY)
VMEM = pl.BlockSpec(memory_space=pltpu.VMEM)


def call(kernel, ins, outs, shapes, scratch, work=0):
    return pl.pallas_call(
        kernel,
        in_specs=ins,
        out_specs=outs,
        out_shape=shapes,
        scratch_shapes=scratch,
        compiler_params=pltpu.CompilerParams(vmem_limit_bytes=VMEM_LIMIT),
        cost_estimate=pl.CostEstimate(flops=work, bytes_accessed=4 << 20, transcendentals=0),
    )


PLANES = (8, 7, FOUR, 8, LANES)
UNITS = (8, 3, SIDE, 8, LANES)
PACK = (7, SIDE, 8, LANES)
WORK = 256 * 1024 * 140


def on_device(support, support_labels, targets, target_labels):
    scratch = pltpu.VMEM
    zx = [[2 * m + core for m in range(16)] for core in range(2)]
    chips = [[2 * chip + core for chip in range(128)] for core in range(2)]
    cores = [(device, device ^ 1) for device in range(32)]

    column_message, row_message = call(
        message_kernel, [VMEM] * 2, [VMEM] * 2, [f32(8, 32, LANES), f32(16, 24, LANES)], []
    )(support.reshape(24, LANES), target_labels.reshape(1, 32))
    columns = lax.all_to_all(column_message, "tgt", 0, 0, tiled=True).reshape(256, LANES)
    planes_t = call(row_kernel, [VMEM], VMEM, f32(*PLANES), [], WORK // 2)(
        targets.transpose(1, 0, 2)
    )
    labels = support_labels.reshape(8, 16, 2).transpose(0, 2, 1).reshape(1, 256)
    columns, planes_t, row_message, labels = lax.optimization_barrier(
        (columns, planes_t, row_message, labels)
    )
    rows = lax.all_to_all(row_message, "sup", 0, 0, tiled=True, axis_index_groups=zx)
    entries_t, pack, inverses, units_t = call(
        target_kernel,
        [VMEM] * 2,
        [VMEM] * 3 + [HBM],
        [f32(8, LANES), f32(*PACK), f32(2, 8, 8, LANES), f32(*UNITS)],
        [
            scratch(UNITS, jnp.float32),
            scratch((8, 1024), jnp.float32),
            pltpu.SemaphoreType.DMA((8,)),
        ],
        WORK,
    )(planes_t, columns)
    rows, entries_t = lax.optimization_barrier((rows, entries_t))
    rows_other = lax.ppermute(rows, "sup", cores)
    payload, planes_s = call(
        entries_kernel,
        [VMEM] * 4,
        [VMEM] * 2,
        [f32(128, FOUR, LANES), f32(*PLANES)],
        [scratch((8, 1024), jnp.float32)],
        WORK // 2,
    )(rows, rows_other, pack, entries_t)
    received = lax.all_to_all(payload, BOTH, 0, 0, tiled=True, axis_index_groups=chips)
    units_s = call(
        units_kernel,
        [VMEM] * 2,
        HBM,
        f32(*UNITS),
        [scratch(UNITS, jnp.float32), pltpu.SemaphoreType.DMA((8,))],
        WORK,
    )(planes_s, pack)
    received, units_s = lax.optimization_barrier((received, units_s))
    received_other = lax.ppermute(received, "sup", cores)
    partial, objective = call(
        solve_kernel,
        [HBM] * 2 + [VMEM] + [HBM] * 6,
        [VMEM] * 2,
        [f32(192, LANES), f32(8, LANES)],
        [
            scratch((2, 512, LANES), jnp.float32),
            scratch((256, LANES), jnp.float32),
            scratch((2, 8, 8, LANES), jnp.float32),
            scratch((16, 3, SIDE, 8, LANES), jnp.float32),
            scratch((16, 3, FOUR, 8, LANES), jnp.float32),
            scratch((256, 256), jnp.float32),
            scratch((256, 256), jnp.float32),
            scratch((3, 256, 256), jnp.bfloat16),
            scratch((3, 256, 256), jnp.bfloat16),
            scratch((2, 256, 256), jnp.bfloat16),
            scratch((16, 8, LANES), jnp.float32),
            scratch((5, 8, 8, LANES), jnp.float32),
            pltpu.SemaphoreType.DMA((8,)),
        ],
        WORK,
    )(
        received.reshape(512, LANES),
        received_other.reshape(512, LANES),
        labels,
        columns,
        inverses,
        units_t,
        units_s,
        planes_t,
        planes_s,
    )
    pieces = lax.all_to_all(partial.reshape(8, 24, LANES), "tgt", 0, 0, tiled=True)
    return jnp.sum(pieces, axis=0).reshape(1, 3, 1024), objective[0, 0]


def solution(mesh):
    placed = (P(BOTH, None, None), P(), P("tgt", None, None), P("tgt"))
    return jax.shard_map(
        on_device,
        mesh=mesh,
        in_specs=placed,
        out_specs=(P(BOTH, None, None), P()),
        check_vma=False,
    )
```

```python
import functools
import math

import jax
import jax.numpy as jnp
from jax import lax
from jax.experimental import pallas as pl
from jax.experimental.pallas import tpu as pltpu
from jax.sharding import PartitionSpec as P

SIDE = 32
CLASSES = 10
BOTH = ("tgt", "sup")
LANES = 128
MAPS = 7 * 32
FOUR = 4
ALPHA1 = (2.0 / 9.0) / (2.0 * math.pi)
ALPHA2 = 1.0 / (2.0 * math.pi)
FIRST = 2.0 / 27.0
SECOND = 2.0 / 9.0
ACOS = (
    1.570796238860342,
    -0.21459108884050843,
    0.08883588680709523,
    -0.04919743925456755,
    0.027762915193263623,
    -0.01200339464235187,
    0.002611719889929782,
)
KIB = 1024
HIGHEST = lax.Precision.HIGHEST


def lane_index(shape):
    return lax.broadcasted_iota(jnp.int32, shape, len(shape) - 1)


def across(x, keep_left, keep_right):
    axis = x.ndim - 1
    return x + pltpu.roll(x, 1, axis) * keep_left + pltpu.roll(x, LANES - 1, axis) * keep_right


def edge_masks(shape):
    column = lane_index(shape) % SIDE
    return (column != 0).astype(jnp.float32), (column != SIDE - 1).astype(jnp.float32)


def pick_blocks(lines, block):
    low = jnp.where(block == 0, lines[0], lines[1])
    return jnp.where(block < 2, low, jnp.where(block == 2, lines[2], lines[3]))


def turned_blocks(lines):
    block = lane_index(lines[0].shape) // SIDE
    result = []
    for k in range(FOUR):
        y = pick_blocks([lines[(p - k) % FOUR] for p in range(FOUR)], block)
        result.append(pltpu.roll(y, LANES - SIDE * k, y.ndim - 1) if k else y)
    return result


def spread_blocks(y):
    lane = lane_index(y.shape)
    low = lane < 64
    even = (lane // SIDE) % 2 == 0
    axis = y.ndim - 1
    turned = pltpu.roll(y, 64, axis)
    first = jnp.where(low, y, turned)
    last = jnp.where(low, turned, y)
    first_turned = pltpu.roll(first, 32, axis)
    last_turned = pltpu.roll(last, 32, axis)
    return (
        jnp.where(even, first, first_turned),
        jnp.where(even, first_turned, first),
        jnp.where(even, last, last_turned),
        jnp.where(even, last_turned, last),
    )


def message_kernel(image_ref, labels_ref, column_ref):
    hot = labels_ref[...].astype(jnp.float32)
    labels = jnp.broadcast_to(jnp.concatenate([hot] * FOUR, axis=1), (8, LANES))
    for d in range(8):
        column_ref[d, pl.ds(0, 24), :] = image_ref[...]
        column_ref[d, pl.ds(24, 8), :] = labels


def column_maps(images_ref, pack_ref):
    keep_left, keep_right = edge_masks((8, LANES))
    for c in range(3):
        for s in range(8):
            y = images_ref[pl.ds(c * 8 + s, 8, stride=32), :]
            for k, z in enumerate(spread_blocks(y)):
                pack_ref[c, 4 * s + k] = z
    sums, variances = {}, {}
    for r in range(SIDE):
        b0, b1, b2 = pack_ref[0, r], pack_ref[1, r], pack_ref[2, r]
        sums[r] = across(b0 * b0 + b1 * b1 + b2 * b2, keep_left, keep_right)
    for r in range(SIDE):
        q = FIRST * vertical(sums, r) + 0.1
        inverse = lax.rsqrt(q)
        pack_ref[3, r] = inverse
        pack_ref[4, r] = q * inverse
        variances[r] = across(q, keep_left, keep_right)
    for r in range(SIDE):
        q = (0.5 * SECOND) * vertical(variances, r) + 0.1
        inverse = lax.rsqrt(q)
        pack_ref[5, r] = inverse
        pack_ref[6, r] = q * inverse


def row_maps(images, rows_ref):
    keep_left, keep_right = edge_masks((8, LANES))
    sublane = lax.broadcasted_iota(jnp.int32, (8, LANES), 0)

    def down(planes):
        above = jnp.where(sublane == 0, 0.0, pltpu.roll(planes[FOUR - 1], 1, 0))
        under = jnp.where(sublane == 7, 0.0, pltpu.roll(planes[0], 7, 0))
        line = [above, *planes, under]
        return [line[k] + line[k + 1] + line[k + 2] for k in range(FOUR)]

    squares = [0.0] * FOUR
    for c in range(3):
        planes = turned_blocks([images(i, c) for i in range(FOUR)])
        for k in range(FOUR):
            rows_ref[c, k] = FIRST * planes[k]
            squares[k] = squares[k] + planes[k] * planes[k]
    squares = [across(x, keep_left, keep_right) for x in squares]
    first = [FIRST * t + 0.1 for t in down(squares)]
    second = [
        (0.5 * SECOND) * t + 0.1 for t in down([across(q, keep_left, keep_right) for q in first])
    ]
    for k in range(FOUR):
        for n, q in ((3, first[k]), (5, second[k])):
            inverse = lax.rsqrt(q)
            rows_ref[n, k] = inverse
            rows_ref[n + 1, k] = q * inverse


def vertical(window, r):
    total = window[r]
    if r > 0:
        total = total + window[r - 1]
    if r < SIDE - 1:
        total = total + window[r + 1]
    return total


def vertical_pair(window, r, offset=None):
    both = window[r] + window[r + 1]
    if offset is not None:
        both = both + offset
    upper = both + window[r - 1] if r > 0 else both
    lower = both + window[r + 2] if r + 2 < SIDE else both
    return upper, lower


def arc(sigma, inverse, scale, alpha, bump):
    raw = sigma * inverse
    if bump is not None:
        raw = raw + bump
    cosine = jnp.clip(raw, -0.9999, 0.9999)
    inside = cosine == raw
    size = jnp.abs(cosine)
    below = 1.0 - size
    poly = jnp.float32(alpha * ACOS[-1])
    for coefficient in ACOS[-2::-1]:
        poly = poly * size + jnp.float32(alpha * coefficient)
    angle = (below * lax.rsqrt(below)) * poly
    slope = jnp.where(cosine >= 0.0, jnp.float32(alpha * math.pi) - angle, angle)
    rest = 1.0 - cosine * cosine
    root = alpha * lax.rsqrt(rest)
    value = scale * (rest * root + slope * cosine)
    return value, slope, root * inverse, inside


def forward_maps(rows_ref, pack_ref, state_ref, bump):
    keep_left, keep_right = edge_masks((8, LANES))

    def row(c, r):
        return jnp.broadcast_to(rows_ref[c, r % FOUR, pl.ds(r // FOUR, 1), :], (8, LANES))

    cross, value_sum, slope_sum = {}, {}, {}
    total = jnp.zeros((8, LANES), jnp.float32)
    for step in range(0, SIDE + 6, 2):
        for r in (step, step + 1):
            if r < SIDE:
                x = sum(row(c, r) * pack_ref[c, r] for c in range(3))
                cross[r] = across(x, keep_left, keep_right)
        base = step - 2
        if 0 <= base < SIDE:
            for r, sigma in zip((base, base + 1), vertical_pair(cross, base, 0.1)):
                inverse = row(3, r) * pack_ref[3, r]
                scale = row(4, r) * pack_ref[4, r]
                value, slope, weight, inside = arc(sigma, inverse, scale, ALPHA1, None)
                product = slope * sigma
                value_sum[r] = across(value, keep_left, keep_right)
                slope_sum[r] = across(product, keep_left, keep_right)
                state_ref[r] = sigma
                state_ref[SIDE + r] = value
                state_ref[2 * SIDE + r] = jnp.where(inside, slope, -slope)
                state_ref[3 * SIDE + r] = jnp.where(inside, sigma * weight, 0.0)
        base = step - 4
        if 0 <= base < SIDE:
            for r, sigma, more in zip(
                (base, base + 1),
                vertical_pair(value_sum, base, 0.1),
                vertical_pair(slope_sum, base),
            ):
                theta = sigma + more
                inverse = row(5, r) * pack_ref[5, r]
                scale = row(6, r) * pack_ref[6, r]
                value, slope, weight, inside = arc(sigma, inverse, scale, ALPHA2, bump)
                total = total + (value + slope * theta)
                dsigma = jnp.where(inside, slope + theta * weight, 0.0)
                state_ref[4 * SIDE + r] = slope
                state_ref[5 * SIDE + r] = dsigma + slope
                state_ref[6 * SIDE + r] = value - dsigma * sigma
    return total


def backward_maps(state_ref, units_ref):
    keep_left, keep_right = edge_masks((8, LANES))
    dslope, dsigma, dtheta = {}, {}, {}
    for step in range(0, SIDE + 6, 2):
        for r in (step, step + 1):
            if r < SIDE:
                dslope[r] = across(state_ref[4 * SIDE + r], keep_left, keep_right)
                dsigma[r] = across(state_ref[5 * SIDE + r], keep_left, keep_right)
        base = step - 2
        if 0 <= base < SIDE:
            for r, dvalue, dproduct in zip(
                (base, base + 1), vertical_pair(dsigma, base), vertical_pair(dslope, base)
            ):
                slope = state_ref[2 * SIDE + r]
                inner = jnp.maximum(slope, 0.0) * dvalue + dproduct * state_ref[3 * SIDE + r]
                squeeze = state_ref[SIDE + r] * dvalue - inner * state_ref[r]
                units_ref[SIDE + r] = squeeze
                dtheta[r] = across(inner + dproduct * jnp.abs(slope), keep_left, keep_right)
        base = step - 4
        if 0 <= base < SIDE:
            for r, unit in zip((base, base + 1), vertical_pair(dtheta, base)):
                units_ref[r] = unit


def sum_entries(totals_ref):
    parts = [part.astype(jnp.float32) for part in split(totals_ref[...] * (2.0 / 1024.0), 3)]
    stacked = jnp.concatenate(parts + [jnp.zeros((8, 1024), jnp.float32)], axis=0)
    source = lax.broadcasted_iota(jnp.int32, (1024, LANES), 0) // SIDE
    pick = (source == lane_index((1024, LANES))).astype(jnp.bfloat16)
    sums = dot(stacked.astype(jnp.bfloat16), pick)
    return sums[:8] + (sums[8:16] + sums[16:24])


def keep_total(totals_ref, group, total):
    totals_ref[:, pl.ds(pl.multiple_of(group * LANES, LANES), LANES)] = total


def keep_planes(planes_ref, state_ref, group):
    for c in range(3):
        for k in range(FOUR):
            state_ref[group, MAPS + FOUR * c + k] = planes_ref[group, c, k]


def own_bump(group):
    image = group * FOUR + lane_index((8, LANES)) // SIDE
    column = lax.broadcasted_iota(jnp.int32, (8, LANES), 0)
    mine = lax.axis_index("sup") // 2
    own = jnp.logical_and(image == mine, column == lax.axis_index("tgt"))
    return own.astype(jnp.float32)


def copy_out(units_ref, units_hbm, sems, group):
    return pltpu.make_async_copy(units_ref.at[group], units_hbm.at[group], sems.at[group])


def row_kernel(images_ref, own_ref, planes_ref, row_ref):
    place = lax.axis_index("sup") // 2 % FOUR
    own = pltpu.roll(own_ref[...], SIDE * place, 1)
    for d in range(row_ref.shape[0]):
        row_ref[d] = own
    for group in range(8):

        def image(i, c, group=group):
            n = group * FOUR + i
            lines = [images_ref[c, pl.ds(n, 1), pl.ds(s * LANES, LANES)] for s in range(8)]
            x = jnp.concatenate(lines, axis=0)
            return pltpu.roll(x, SIDE * i, 1) if i else x

        row_maps(image, planes_ref.at[group])


def target_kernel(
    planes_ref,
    columns_ref,
    entries_ref,
    pack_ref,
    state_hbm,
    state_ref,
    totals_ref,
    sems,
):
    column_maps(columns_ref, pack_ref)

    def body(group, carry):
        total = forward_maps(planes_ref.at[group], pack_ref, state_ref.at[group], None)
        keep_total(totals_ref, group, total)
        keep_planes(planes_ref, state_ref, group)
        copy_out(state_ref, state_hbm, sems, group).start()
        return carry

    lax.fori_loop(0, 8, body, 0)
    entries_ref[...] = sum_entries(totals_ref)
    for group in range(8):
        copy_out(state_ref, state_hbm, sems, group).wait()


def entries_kernel(
    own_ref,
    other_ref,
    pack_ref,
    entries_t_ref,
    payload_ref,
    state_hbm,
    planes_ref,
    state_ref,
    totals_ref,
    sems,
):
    for half, images_ref in enumerate((own_ref, other_ref)):
        for group in range(FOUR):
            row_maps(
                lambda i, c: images_ref[group * FOUR + i, pl.ds(c * 8, 8), :],
                planes_ref.at[half * FOUR + group],
            )

    def body(group, carry):
        total = forward_maps(
            planes_ref.at[group], pack_ref, state_ref.at[group], own_bump(group)
        )
        keep_total(totals_ref, group, total)
        keep_planes(planes_ref, state_ref, group)
        copy_out(state_ref, state_hbm, sems, group).start()
        return carry

    lax.fori_loop(0, 8, body, 0)
    entries = sum_entries(totals_ref)
    lane = lane_index((8, LANES))
    turned = jnp.where(lane < 16, pltpu.roll(entries, LANES - 16, 1), pltpu.roll(entries, 16, 1))
    turned = jnp.where(lane < SIDE, turned, 0.0)
    entries = jnp.where(lax.axis_index("sup") % 2 == 1, turned, entries)
    both = entries + pltpu.roll(entries_t_ref[...], SIDE, 1)
    both = both + pltpu.roll(pltpu.roll(both, 64, 1), FOUR, 0)
    both = pltpu.roll(both, SIDE * (lax.axis_index("tgt") % FOUR), 1)
    for d in range(payload_ref.shape[0]):
        payload_ref[d] = both[:FOUR]
    for group in range(8):
        copy_out(state_ref, state_hbm, sems, group).wait()


def units_kernel(state_t_hbm, state_s_hbm, units_hbm, state_ref, units_ref, in_sems, out_sems):
    def copy_in(place, source, group):
        return pltpu.make_async_copy(
            source.at[group, pl.ds(0, 6 * SIDE)], state_ref.at[place], in_sems.at[place]
        )

    parts = ((0, state_t_hbm), (8, state_s_hbm))
    for place, source in parts:
        for group in range(8):
            copy_in(place + group, source, group).start()

    for place, source in parts:

        def body(group, carry, place=place, source=source):
            copy_in(place + group, source, group).wait()
            backward_maps(state_ref.at[place + group], units_ref.at[place + group])
            copy_out(units_ref, units_hbm, out_sems, place + group).start()
            return carry

        lax.fori_loop(0, 8, body, 0)
    for group in range(16):
        copy_out(units_ref, units_hbm, out_sems, group).wait()


def dot(a, b):
    return jnp.dot(a, b, preferred_element_type=jnp.float32)


def dot_nt(a, b):
    return lax.dot_general(a, b, (((1,), (1,)), ((), ())), preferred_element_type=jnp.float32)


def split(x, parts):
    result = []
    for _ in range(parts):
        result.append(x.astype(jnp.bfloat16))
        x = x - result[-1].astype(jnp.float32)
    return result


def product3(a, b):
    (ah, al), (bh, bl) = a, b
    return dot(ah, bh) + (dot(ah, bl) + dot(al, bh))


def thin_exact(a, b, product=dot):
    high, middle, low = split(a, 3)
    first = product(jnp.concatenate([high, middle, low], axis=0), b[0])
    second = product(jnp.concatenate([high, middle], axis=0), b[1])
    third = product(high, b[2])
    small = first[32:48] + second[16:32] + third
    return first[:16] + (first[16:32] + second[:16] + small)


def thin_near(a, b):
    high, middle = split(a, 2)
    first = dot(jnp.concatenate([high, middle], axis=0), b[0])
    return first[:16] + (first[16:] + dot(high, b[1]))


def merge_blocks(lines, block):
    total = pick_blocks(lines, block)
    for d in range(1, FOUR):
        moved = pick_blocks([lines[(k - d) % FOUR] for k in range(FOUR)], block)
        total = total + pltpu.roll(moved, LANES - SIDE * d, 1)
    return total


def image_stencil(lines, masks, block):
    lines = [across(x, *masks) for x in lines]
    ups = [pltpu.roll(x, SIDE, 1) for x in lines]
    downs = [pltpu.roll(x, LANES - SIDE, 1) for x in lines]
    zero = jnp.zeros_like(lines[0])
    result = []
    for s in range(8):
        up = jnp.where(block == 0, ups[s - 1] if s else zero, ups[s])
        down = jnp.where(block == 3, downs[s + 1] if s < 7 else zero, downs[s])
        result.append(lines[s] + up + down)
    return result


def solve_kernel(
    own_ref,
    other_ref,
    support_labels_ref,
    columns_ref,
    pack_hbm,
    units_hbm,
    state_t_hbm,
    state_s_hbm,
    grad_hbm,
    objective_ref,
    grad_ref,
    inverses_ref,
    units_ref,
    second_ref,
    kernel_ref,
    inverse_ref,
    matrix_parts,
    cross_parts,
    inverse_parts,
    weights_ref,
    grads_ref,
    sems,
):
    core = lax.axis_index("sup") % 2
    copies = [
        pltpu.make_async_copy(source, target, sems.at[n])
        for n, (source, target) in enumerate(
            [
                (pack_hbm.at[3], inverses_ref.at[0]),
                (pack_hbm.at[5], inverses_ref.at[1]),
                (units_hbm, units_ref),
                (state_t_hbm.at[:, pl.ds(6 * SIDE, SIDE + 12)], second_ref.at[pl.ds(0, 8)]),
                (state_s_hbm.at[:, pl.ds(6 * SIDE, SIDE + 12)], second_ref.at[pl.ds(8, 8)]),
            ]
        )
    ]
    for copy in copies:
        copy.start()

    count = 256
    for half, source_ref in enumerate((own_ref, other_ref)):
        first = 16 * (core if half == 0 else 1 - core)
        for j in range(FOUR):
            for h in range(2):
                blocks = []
                for i in range(FOUR):
                    start = (FOUR * h + i) * 16 * FOUR + j
                    blocks.append(source_ref[pl.ds(start, 16, stride=FOUR), :])
                for b, y in enumerate(turned_blocks(blocks)):
                    start = (FOUR * (b // 2) + j) * 32 + first
                    rows = pl.ds(pl.multiple_of(start, 16), 16)
                    lanes = pl.ds(h * LANES, LANES)
                    if b % 2 == 0:
                        kernel_ref[rows, lanes] = y
                    else:
                        for n, part in enumerate(split(y, 3)):
                            cross_parts[n, rows, lanes] = part

    matrix = kernel_ref[...]
    row_id = lax.broadcasted_iota(jnp.int32, (count, count), 0)
    col_id = lax.broadcasted_iota(jnp.int32, (count, count), 1)
    eye = row_id == col_id
    trace = jnp.sum(jnp.where(eye, matrix, 0.0))
    ridge = 0.1 * trace / count
    matrix = matrix + jnp.where(eye, ridge, 0.0)
    for n, part in enumerate(split(matrix, 3)):
        matrix_parts[n] = part

    def whole(x):
        return jnp.sum(x, axis=1, keepdims=True)

    v_row, v_col = jnp.sum(matrix, axis=0, keepdims=True), whole(matrix)
    norm = lax.rsqrt(whole(v_row * v_row))
    v_row, v_col = v_row * norm, v_col * norm
    w_row, w_col = jnp.sum(matrix * v_col, axis=0, keepdims=True), whole(matrix * v_row)
    top = whole(w_row * v_row)
    off = w_row - top * v_row
    rest = jnp.sum(jnp.abs(matrix - (top * v_col) * v_row), axis=0, keepdims=True)
    rest = jnp.max(rest, axis=1, keepdims=True)
    alpha = 2.0 / (rest + ridge)
    limit = jnp.maximum(alpha * rest, 1.0) + jnp.sqrt(alpha / top * whole(off * off))
    floor = alpha * ridge
    scale = 2.0 / (limit + floor)
    spread = (limit - floor) / (limit + floor)
    square = spread * spread
    gain = 2.0 / (2.0 - square)
    gamma = scale * (1.0 / top - alpha)
    alpha = scale * alpha
    side = gain * ((2.0 * gamma - gamma * gamma * top) * v_col - (alpha * gamma) * w_col)
    inverse_ref[...] = (
        jnp.where(eye, 2.0 * gain * alpha, 0.0)
        - (gain * alpha * alpha) * matrix
        + side * v_row
        - (gain * alpha * gamma * v_col) * w_row
    )
    square = square[0, 0]

    def improve(delta):
        square = delta * delta
        gain = 2.0 / (2.0 - square)
        x = inverse_ref[...]
        parts = split(x, 2)
        error = jnp.where(eye, 1.0, 0.0) - product3((matrix_parts[0], matrix_parts[1]), parts)
        inverse_ref[...] = gain * (x + product3(parts, split(error, 2)))
        return square / (2.0 - square)

    lax.while_loop(lambda delta: delta > 1e-3, improve, square / (2.0 - square))
    for n, part in enumerate(split(inverse_ref[...], 2)):
        inverse_parts[n] = part

    class_id = lax.broadcasted_iota(jnp.int32, (16, count), 0)

    def one_hot(labels):
        hot = (class_id == labels).astype(jnp.float32) - 0.1
        return jnp.where(class_id < CLASSES, hot, 0.0)

    support_hot = one_hot(support_labels_ref[...])
    lane1 = lane_index((1, LANES))
    halves = []
    for h in range(2):
        line = [columns_ref[pl.ds((FOUR * h + i) * 32 + 24, 1), :] for i in range(FOUR)]
        line = [jnp.where(lane1 // SIDE == i, x, 0.0) for i, x in enumerate(line)]
        halves.append((line[0] + line[1]) + (line[2] + line[3]))
    target_labels = jnp.concatenate(halves, axis=1).astype(jnp.int32)
    target_hot = one_hot(target_labels)

    def refine(coeffs, adjoint):
        step = thin_near(support_hot - thin_exact(coeffs, matrix_parts), inverse_parts)
        coeffs = coeffs + step
        residual = thin_exact(coeffs, cross_parts) - target_hot
        right = thin_exact(residual, cross_parts, dot_nt)
        if adjoint is None:
            adjoint = thin_near(right, inverse_parts)
        more = thin_near(right - thin_exact(adjoint, matrix_parts), inverse_parts)
        adjoint = adjoint + more
        moved = jnp.maximum(
            whole(jnp.sum(step * step, axis=0, keepdims=True))
            / whole(jnp.sum(coeffs * coeffs, axis=0, keepdims=True)),
            whole(jnp.sum(more * more, axis=0, keepdims=True))
            / whole(jnp.sum(adjoint * adjoint, axis=0, keepdims=True)),
        )
        return coeffs, adjoint, residual, moved

    coeffs, adjoint, residual, moved = refine(thin_near(support_hot, inverse_parts), None)

    def again(state):
        coeffs, adjoint, _, moved, _, rounds = state
        coeffs, adjoint, residual, now = refine(coeffs, adjoint)
        return coeffs, adjoint, residual, now, (now * now / moved)[0, 0], rounds + 1

    coeffs, adjoint, residual, _, _, _ = lax.while_loop(
        lambda state: jnp.logical_and(state[4] > 1e-13, state[5] < 40),
        again,
        (coeffs, adjoint, residual, moved, (moved * moved)[0, 0], 0),
    )
    objective_ref[...] = jnp.full((8, LANES), 0.5 * jnp.sum(residual * residual), jnp.float32)
    trace_grad = -jnp.sum(adjoint * coeffs)

    mine_t = lax.axis_index("tgt")
    mine = core * 16 + lax.axis_index("sup") // 2
    coeff_parts, adjoint_parts = split(coeffs, 3), split(adjoint, 3)
    ids = lax.broadcasted_iota(jnp.int32, (16, count), 1)
    wanted = lax.broadcasted_iota(jnp.int32, (16, count), 0) * 32 + mine
    picked = dot_nt(
        (ids == wanted).astype(jnp.bfloat16), jnp.concatenate(coeff_parts + adjoint_parts, axis=0)
    ).astype(jnp.bfloat16)
    turn = lax.rem(count - 32 * mine_t, count)

    def row_parts(x):
        return split(pltpu.roll(x, turn, 1)[:, :LANES], 3)

    zero = jnp.zeros((48, LANES), jnp.bfloat16)
    pairs = 0.0
    for c, a, r in zip(row_parts(-coeffs), row_parts(-adjoint), row_parts(residual)):
        side_s = jnp.concatenate([a, a, a, c, c, c], axis=0)
        side_t = jnp.concatenate([r, r, r, zero], axis=0)
        pairs = pairs + dot(picked, jnp.concatenate([side_s, side_t], axis=1))
    sub8 = lax.broadcasted_iota(jnp.int32, (8, LANES), 0)
    lane8 = lane_index((8, LANES))
    own = jnp.logical_and(sub8 == mine_t, lane8 == mine)
    pairs_s = pairs[:8, :LANES] + jnp.where(own, (0.2 / count) * trace_grad, 0.0)
    pairs = jnp.concatenate([pairs[:8, LANES:], pairs_s], axis=0)
    pairs = jnp.where(lane_index((16, LANES)) < SIDE, pairs * (2.0 / 1024.0), 0.0)
    high, middle, low = [part.astype(jnp.float32) for part in split(pairs, 3)]
    stacked = high + pltpu.roll(middle, 32, 1) + pltpu.roll(low, 64, 1)
    widen = lax.broadcasted_iota(jnp.int32, (LANES, 1024), 0) % SIDE
    widen = widen == lax.broadcasted_iota(jnp.int32, (LANES, 1024), 1) // SIDE
    wide = dot(stacked.astype(jnp.bfloat16), widen.astype(jnp.bfloat16))
    for g in range(8):
        weights_ref[g] = wide[:8, g * LANES : (g + 1) * LANES]
        weights_ref[8 + lax.rem(g + FOUR * core, 8)] = wide[8:, g * LANES : (g + 1) * LANES]

    for copy in copies:
        copy.wait()

    block = lane8 // SIDE

    def gather_line(s, carry):
        lines = [[] for _ in range(5)]
        for k in range(FOUR):
            r = s * FOUR + k
            sums = [None] * 5
            for g in range(16):
                weight = weights_ref[g]
                dx = weight * units_ref[g, r]
                terms = [
                    dx
                    * jnp.broadcast_to(
                        second_ref[g, SIDE + FOUR * c + k, pl.ds(s, 1), :], (8, LANES)
                    )
                    for c in range(3)
                ]
                terms.append(weight * units_ref[g, SIDE + r])
                terms.append(weight * second_ref[g, r])
                sums = [t if a is None else a + t for a, t in zip(sums, terms)]
            for n in range(5):
                lines[n].append(sums[n])
        for n in range(5):
            grads_ref[n, s] = merge_blocks(lines[n], block)
        return carry

    lax.fori_loop(0, 8, gather_line, 0, unroll=4)

    masks = edge_masks((8, LANES))

    def half_over_variance(n, s):
        inverse = pick_blocks([inverses_ref[n, FOUR * s + k] for k in range(FOUR)], block)
        return 0.5 * inverse * inverse

    second = [half_over_variance(1, s) * grads_ref[4, s] for s in range(8)]
    second = image_stencil(second, masks, block)
    first = [
        half_over_variance(0, s) * grads_ref[3, s] + (0.5 * SECOND) * second[s] for s in range(8)
    ]
    first = image_stencil(first, masks, block)
    for s in range(8):
        for c in range(3):
            image = columns_ref[pl.ds(c * 8 + s, 8, stride=32), :]
            grad_ref[pl.ds(c * 8 + s, 8, stride=24), :] = (
                grads_ref[c, s] + (2.0 * FIRST) * first[s] * image
            )
    copy = pltpu.make_async_copy(grad_ref, grad_hbm, sems.at[5])
    copy.start()
    copy.wait()


def f32(*shape):
    return jax.ShapeDtypeStruct(shape, jnp.float32)


HBM = pl.BlockSpec(memory_space=pltpu.HBM)
VMEM = pl.BlockSpec(memory_space=pltpu.VMEM)


def call(kernel, ins, outs, shapes, scratch, limit, work=0):
    return pl.pallas_call(
        kernel,
        in_specs=ins,
        out_specs=outs,
        out_shape=shapes,
        scratch_shapes=scratch,
        compiler_params=pltpu.CompilerParams(vmem_limit_bytes=limit * KIB),
        cost_estimate=pl.CostEstimate(flops=work, bytes_accessed=4 << 20, transcendentals=0),
    )


PLANES = (8, 7, FOUR, 8, LANES)
STATE = (8, MAPS + 12, 8, LANES)
UNITS = (16, 2 * SIDE, 8, LANES)
PACK = (7, SIDE, 8, LANES)
WORK = 256 * 1024 * 140


def on_device(support, support_labels, targets, target_labels):
    scratch = pltpu.VMEM
    zx = [[2 * m + core for m in range(16)] for core in range(2)]
    chips = [[2 * chip + core for chip in range(128)] for core in range(2)]
    cores = [(device, device ^ 1) for device in range(32)]

    image = support.reshape(24, LANES)
    column_message = call(
        message_kernel, [VMEM] * 2, VMEM, f32(8, 32, LANES), [], 60 * KIB
    )(image, target_labels.reshape(1, 32))
    columns = lax.all_to_all(column_message, "tgt", 0, 0, tiled=True).reshape(256, LANES)
    planes_t, row_message = call(
        row_kernel, [VMEM] * 2, [VMEM] * 2, [f32(*PLANES), f32(16, 24, LANES)], [], 48 * KIB, WORK // 2
    )(targets.transpose(1, 0, 2), image)
    labels = support_labels.reshape(8, 16, 2).transpose(0, 2, 1).reshape(1, 256)
    columns, planes_t, row_message, labels = lax.optimization_barrier(
        (columns, planes_t, row_message, labels)
    )
    rows = lax.all_to_all(row_message, "sup", 0, 0, tiled=True, axis_index_groups=zx)
    entries_t, pack, state_t = call(
        target_kernel,
        [VMEM] * 2,
        [VMEM] * 2 + [HBM],
        [f32(8, LANES), f32(*PACK), f32(*STATE)],
        [
            scratch(STATE, jnp.float32),
            scratch((8, 1024), jnp.float32),
            pltpu.SemaphoreType.DMA((8,)),
        ],
        51500,
        WORK,
    )(planes_t, columns)
    rows, entries_t = lax.optimization_barrier((rows, entries_t))
    rows_other = lax.ppermute(rows, "sup", cores)
    payload, state_s = call(
        entries_kernel,
        [VMEM] * 4,
        [VMEM, HBM],
        [f32(128, FOUR, LANES), f32(*STATE)],
        [
            scratch(PLANES, jnp.float32),
            scratch(STATE, jnp.float32),
            scratch((8, 1024), jnp.float32),
            pltpu.SemaphoreType.DMA((8,)),
        ],
        52500,
        WORK // 2,
    )(rows, rows_other, pack, entries_t)
    received = lax.all_to_all(payload, BOTH, 0, 0, tiled=True, axis_index_groups=chips)
    units = call(
        units_kernel,
        [HBM] * 2,
        HBM,
        f32(*UNITS),
        [
            scratch((16, 6 * SIDE, 8, LANES), jnp.float32),
            scratch(UNITS, jnp.float32),
            pltpu.SemaphoreType.DMA((16,)),
            pltpu.SemaphoreType.DMA((16,)),
        ],
        54200,
        WORK,
    )(state_t, state_s)
    received, units = lax.optimization_barrier((received, units))
    received_other = lax.ppermute(received, "sup", cores)
    partial, objective = call(
        solve_kernel,
        [VMEM] * 4 + [HBM] * 4,
        [HBM, VMEM],
        [f32(192, LANES), f32(8, LANES)],
        [
            scratch((192, LANES), jnp.float32),
            scratch((2, SIDE, 8, LANES), jnp.float32),
            scratch((16, 2 * SIDE, 8, LANES), jnp.float32),
            scratch((16, SIDE + 12, 8, LANES), jnp.float32),
            scratch((256, 256), jnp.float32),
            scratch((256, 256), jnp.float32),
            scratch((3, 256, 256), jnp.bfloat16),
            scratch((3, 256, 256), jnp.bfloat16),
            scratch((2, 256, 256), jnp.bfloat16),
            scratch((16, 8, LANES), jnp.float32),
            scratch((5, 8, 8, LANES), jnp.float32),
            pltpu.SemaphoreType.DMA((6,)),
        ],
        54200,
        WORK,
    )(
        received.reshape(512, LANES),
        received_other.reshape(512, LANES),
        labels,
        columns,
        pack,
        units,
        state_t,
        state_s,
    )
    pieces = lax.all_to_all(partial.reshape(8, 24, LANES), "tgt", 0, 0, tiled=True)
    return jnp.sum(pieces, axis=0).reshape(1, 3, 1024), objective[0, 0]


def solution(mesh):
    placed = (P(BOTH, None, None), P(), P("tgt", None, None), P("tgt"))
    return jax.shard_map(
        on_device,
        mesh=mesh,
        in_specs=placed,
        out_specs=(P(BOTH, None, None), P()),
        check_vma=False,
    )
```

```python
import functools
import math

import jax
import jax.numpy as jnp
from jax import lax
from jax.experimental import pallas as pl
from jax.experimental.pallas import tpu as pltpu
from jax.sharding import PartitionSpec as P

SIDE = 32
CLASSES = 10
BOTH = ("tgt", "sup")
LANES = 128
MAPS = 7 * 32
FOUR = 4
ALPHA1 = (2.0 / 9.0) / (2.0 * math.pi)
ALPHA2 = 1.0 / (2.0 * math.pi)
FIRST = 2.0 / 27.0
SECOND = 2.0 / 9.0
ACOS = (
    1.570796238860342,
    -0.21459108884050843,
    0.08883588680709523,
    -0.04919743925456755,
    0.027762915193263623,
    -0.01200339464235187,
    0.002611719889929782,
)
KIB = 1024
HIGHEST = lax.Precision.HIGHEST


def lane_index(shape):
    return lax.broadcasted_iota(jnp.int32, shape, len(shape) - 1)


def across(x, keep_left, keep_right):
    axis = x.ndim - 1
    return x + pltpu.roll(x, 1, axis) * keep_left + pltpu.roll(x, LANES - 1, axis) * keep_right


def edge_masks(shape):
    column = lane_index(shape) % SIDE
    return (column != 0).astype(jnp.float32), (column != SIDE - 1).astype(jnp.float32)


def pick_blocks(lines, block):
    low = jnp.where(block == 0, lines[0], lines[1])
    return jnp.where(block < 2, low, jnp.where(block == 2, lines[2], lines[3]))


def turned_blocks(lines):
    block = lane_index(lines[0].shape) // SIDE
    result = []
    for k in range(FOUR):
        y = pick_blocks([lines[(p - k) % FOUR] for p in range(FOUR)], block)
        result.append(pltpu.roll(y, LANES - SIDE * k, y.ndim - 1) if k else y)
    return result


def spread_blocks(y):
    lane = lane_index(y.shape)
    low = lane < 64
    even = (lane // SIDE) % 2 == 0
    axis = y.ndim - 1
    turned = pltpu.roll(y, 64, axis)
    first = jnp.where(low, y, turned)
    last = jnp.where(low, turned, y)
    first_turned = pltpu.roll(first, 32, axis)
    last_turned = pltpu.roll(last, 32, axis)
    return (
        jnp.where(even, first, first_turned),
        jnp.where(even, first_turned, first),
        jnp.where(even, last, last_turned),
        jnp.where(even, last_turned, last),
    )


def message_kernel(image_ref, labels_ref, column_ref, row_ref):
    hot = labels_ref[...].astype(jnp.float32)
    labels = jnp.broadcast_to(jnp.concatenate([hot] * FOUR, axis=1), (8, LANES))
    image = image_ref[...]
    for d in range(column_ref.shape[0]):
        column_ref[d, pl.ds(0, 24), :] = image
        column_ref[d, pl.ds(24, 8), :] = labels
    turned = pltpu.roll(image, SIDE * (lax.axis_index("sup") // 2 % FOUR), 1)
    for d in range(row_ref.shape[0]):
        row_ref[d] = turned


def column_maps(images_ref, pack_ref):
    keep_left, keep_right = edge_masks((8, LANES))
    for c in range(3):
        for s in range(8):
            y = images_ref[pl.ds(c * 8 + s, 8, stride=32), :]
            for k, z in enumerate(spread_blocks(y)):
                pack_ref[c, 4 * s + k] = z
    sums, variances = {}, {}
    for r in range(SIDE):
        b0, b1, b2 = pack_ref[0, r], pack_ref[1, r], pack_ref[2, r]
        sums[r] = across(b0 * b0 + b1 * b1 + b2 * b2, keep_left, keep_right)
    for r in range(SIDE):
        q = FIRST * vertical(sums, r) + 0.1
        inverse = lax.rsqrt(q)
        pack_ref[3, r] = inverse
        pack_ref[4, r] = q * inverse
        variances[r] = across(q, keep_left, keep_right)
    for r in range(SIDE):
        q = (0.5 * SECOND) * vertical(variances, r) + 0.1
        inverse = lax.rsqrt(q)
        pack_ref[5, r] = inverse
        pack_ref[6, r] = q * inverse


def row_maps(images, rows_ref):
    keep_left, keep_right = edge_masks((8, LANES))
    sublane = lax.broadcasted_iota(jnp.int32, (8, LANES), 0)

    def down(planes):
        above = jnp.where(sublane == 0, 0.0, pltpu.roll(planes[FOUR - 1], 1, 0))
        under = jnp.where(sublane == 7, 0.0, pltpu.roll(planes[0], 7, 0))
        line = [above, *planes, under]
        return [line[k] + line[k + 1] + line[k + 2] for k in range(FOUR)]

    squares = [0.0] * FOUR
    for c in range(3):
        planes = turned_blocks([images(i, c) for i in range(FOUR)])
        for k in range(FOUR):
            rows_ref[c, k] = FIRST * planes[k]
            squares[k] = squares[k] + planes[k] * planes[k]
    squares = [across(x, keep_left, keep_right) for x in squares]
    first = [FIRST * t + 0.1 for t in down(squares)]
    second = [
        (0.5 * SECOND) * t + 0.1 for t in down([across(q, keep_left, keep_right) for q in first])
    ]
    for k in range(FOUR):
        for n, q in ((3, first[k]), (5, second[k])):
            inverse = lax.rsqrt(q)
            rows_ref[n, k] = inverse
            rows_ref[n + 1, k] = q * inverse


def vertical(window, r):
    total = window[r]
    if r > 0:
        total = total + window[r - 1]
    if r < SIDE - 1:
        total = total + window[r + 1]
    return total


def vertical_pair(window, r, offset=None):
    both = window[r] + window[r + 1]
    if offset is not None:
        both = both + offset
    upper = both + window[r - 1] if r > 0 else both
    lower = both + window[r + 2] if r + 2 < SIDE else both
    return upper, lower


def arc(sigma, inverse, scale, alpha, bump):
    raw = sigma * inverse
    if bump is not None:
        raw = raw + bump
    cosine = jnp.clip(raw, -0.9999, 0.9999)
    inside = cosine == raw
    size = jnp.abs(cosine)
    below = 1.0 - size
    poly = jnp.float32(alpha * ACOS[-1])
    for coefficient in ACOS[-2::-1]:
        poly = poly * size + jnp.float32(alpha * coefficient)
    angle = (below * lax.rsqrt(below)) * poly
    slope = jnp.where(cosine >= 0.0, jnp.float32(alpha * math.pi) - angle, angle)
    rest = 1.0 - cosine * cosine
    root = alpha * lax.rsqrt(rest)
    value = scale * (rest * root + slope * cosine)
    return value, slope, root * inverse, inside


def forward_maps(rows_ref, pack_ref, state_ref, bump):
    keep_left, keep_right = edge_masks((8, LANES))

    def row(c, r):
        return jnp.broadcast_to(rows_ref[c, r % FOUR, pl.ds(r // FOUR, 1), :], (8, LANES))

    cross, value_sum, slope_sum = {}, {}, {}
    total = jnp.zeros((8, LANES), jnp.float32)
    for step in range(0, SIDE + 6, 2):
        for r in (step, step + 1):
            if r < SIDE:
                x = row(0, r) * pack_ref[0, r] + row(1, r) * pack_ref[1, r]
                x = x + row(2, r) * pack_ref[2, r]
                cross[r] = across(x, keep_left, keep_right)
        base = step - 2
        if 0 <= base < SIDE:
            for r, sigma in zip((base, base + 1), vertical_pair(cross, base, 0.1)):
                inverse = row(3, r) * pack_ref[3, r]
                scale = row(4, r) * pack_ref[4, r]
                value, slope, weight, inside = arc(sigma, inverse, scale, ALPHA1, None)
                product = slope * sigma
                value_sum[r] = across(value, keep_left, keep_right)
                slope_sum[r] = across(product, keep_left, keep_right)
                state_ref[r] = sigma
                state_ref[SIDE + r] = value
                state_ref[2 * SIDE + r] = jnp.where(inside, slope, -slope)
                state_ref[3 * SIDE + r] = jnp.where(inside, sigma * weight, 0.0)
        base = step - 4
        if 0 <= base < SIDE:
            for r, sigma, more in zip(
                (base, base + 1),
                vertical_pair(value_sum, base, 0.1),
                vertical_pair(slope_sum, base),
            ):
                theta = sigma + more
                inverse = row(5, r) * pack_ref[5, r]
                scale = row(6, r) * pack_ref[6, r]
                value, slope, weight, inside = arc(sigma, inverse, scale, ALPHA2, bump)
                total = total + (value + slope * theta)
                dsigma = jnp.where(inside, slope + theta * weight, 0.0)
                state_ref[4 * SIDE + r] = slope
                state_ref[5 * SIDE + r] = dsigma + slope
                state_ref[6 * SIDE + r] = value - dsigma * sigma
    return total


def backward_maps(state_ref, units_ref):
    keep_left, keep_right = edge_masks((8, LANES))
    dslope, dsigma, dtheta = {}, {}, {}
    for step in range(0, SIDE + 6, 2):
        for r in (step, step + 1):
            if r < SIDE:
                dslope[r] = across(state_ref[4 * SIDE + r], keep_left, keep_right)
                dsigma[r] = across(state_ref[5 * SIDE + r], keep_left, keep_right)
        base = step - 2
        if 0 <= base < SIDE:
            for r, dvalue, dproduct in zip(
                (base, base + 1), vertical_pair(dsigma, base), vertical_pair(dslope, base)
            ):
                slope = state_ref[2 * SIDE + r]
                inner = jnp.maximum(slope, 0.0) * dvalue + dproduct * state_ref[3 * SIDE + r]
                squeeze = state_ref[SIDE + r] * dvalue - inner * state_ref[r]
                units_ref[SIDE + r] = squeeze
                dtheta[r] = across(inner + dproduct * jnp.abs(slope), keep_left, keep_right)
        base = step - 4
        if 0 <= base < SIDE:
            for r, unit in zip((base, base + 1), vertical_pair(dtheta, base)):
                units_ref[r] = unit


def sum_entries(totals_ref):
    parts = [part.astype(jnp.float32) for part in split(totals_ref[...] * (2.0 / 1024.0), 3)]
    stacked = jnp.concatenate(parts + [jnp.zeros((8, 1024), jnp.float32)], axis=0)
    source = lax.broadcasted_iota(jnp.int32, (1024, LANES), 0) // SIDE
    pick = (source == lane_index((1024, LANES))).astype(jnp.bfloat16)
    sums = dot(stacked.astype(jnp.bfloat16), pick)
    return sums[:8] + (sums[8:16] + sums[16:24])


def keep_total(totals_ref, group, total):
    totals_ref[:, pl.ds(pl.multiple_of(group * LANES, LANES), LANES)] = total


def keep_planes(planes_ref, group, state_ref, place):
    for c in range(3):
        for k in range(FOUR):
            state_ref[place, MAPS + FOUR * c + k] = planes_ref[group, c, k]


def own_bump(group):
    image = group * FOUR + lane_index((8, LANES)) // SIDE
    column = lax.broadcasted_iota(jnp.int32, (8, LANES), 0)
    mine = lax.axis_index("sup") // 2
    own = jnp.logical_and(image == mine, column == lax.axis_index("tgt"))
    return own.astype(jnp.float32)


def copy_out(units_ref, units_hbm, sems, group):
    return pltpu.make_async_copy(units_ref.at[group], units_hbm.at[group], sems.at[group])


def row_kernel(images_ref, planes_ref):
    for group in range(8):

        def image(i, c, group=group):
            n = group * FOUR + i
            lines = [images_ref[c, pl.ds(n, 1), pl.ds(s * LANES, LANES)] for s in range(8)]
            x = jnp.concatenate(lines, axis=0)
            return pltpu.roll(x, SIDE * i, 1) if i else x

        row_maps(image, planes_ref.at[group])


def target_kernel(
    planes_ref,
    columns_ref,
    entries_ref,
    pack_ref,
    state_hbm,
    state_ref,
    totals_ref,
    sems,
):
    column_maps(columns_ref, pack_ref)

    def body(group, carry):
        total = forward_maps(planes_ref.at[group], pack_ref, state_ref.at[group], None)
        keep_total(totals_ref, group, total)
        keep_planes(planes_ref, group, state_ref, group)
        copy_out(state_ref, state_hbm, sems, group).start()
        return carry

    lax.fori_loop(0, 8, body, 0)
    entries_ref[...] = sum_entries(totals_ref)
    for group in range(8):
        copy_out(state_ref, state_hbm, sems, group).wait()


def half_kernel(images_ref, planes_ref):
    for group in range(FOUR):
        row_maps(
            lambda i, c: images_ref[group * FOUR + i, pl.ds(c * 8, 8), :], planes_ref.at[group]
        )


def entries_kernel(
    planes_own_ref,
    other_ref,
    pack_ref,
    entries_t_ref,
    payload_hbm,
    state_hbm,
    planes_ref,
    state_ref,
    totals_ref,
    payload_ref,
    sems,
):
    half_kernel(other_ref, planes_ref)

    def own_body(group, carry):
        total = forward_maps(
            planes_own_ref.at[group], pack_ref, state_ref.at[group], own_bump(group)
        )
        keep_total(totals_ref, group, total)
        keep_planes(planes_own_ref, group, state_ref, group)
        copy_out(state_ref, state_hbm, sems, group).start()
        return carry

    def other_body(group, carry):
        place = FOUR + group
        total = forward_maps(planes_ref.at[group], pack_ref, state_ref.at[place], None)
        keep_total(totals_ref, place, total)
        keep_planes(planes_ref, group, state_ref, place)
        copy_out(state_ref, state_hbm, sems, place).start()
        return carry

    lax.fori_loop(0, FOUR, own_body, 0)
    lax.fori_loop(0, FOUR, other_body, 0)
    entries = sum_entries(totals_ref)
    lane = lane_index((8, LANES))
    turned = jnp.where(lane < 16, pltpu.roll(entries, LANES - 16, 1), pltpu.roll(entries, 16, 1))
    turned = jnp.where(lane < SIDE, turned, 0.0)
    entries = jnp.where(lax.axis_index("sup") % 2 == 1, turned, entries)
    both = entries + pltpu.roll(entries_t_ref[...], SIDE, 1)
    both = both + pltpu.roll(pltpu.roll(both, 64, 1), FOUR, 0)
    both = pltpu.roll(both, SIDE * (lax.axis_index("tgt") % FOUR), 1)
    both = jnp.concatenate([both[:FOUR], both[:FOUR]], axis=0)
    for d in range(payload_ref.shape[0] // 8):
        payload_ref[pl.ds(8 * d, 8), :] = both
    payload_out = pltpu.make_async_copy(payload_ref, payload_hbm, sems.at[8])
    payload_out.start()
    for group in range(8):
        copy_out(state_ref, state_hbm, sems, group).wait()
    payload_out.wait()


def units_kernel(state_t_hbm, state_s_hbm, units_hbm, state_ref, units_ref, in_sems, out_sems):
    def copy_in(place, source, group):
        return pltpu.make_async_copy(
            source.at[group, pl.ds(0, 6 * SIDE)], state_ref.at[place], in_sems.at[place]
        )

    parts = ((0, state_t_hbm), (8, state_s_hbm))
    for place, source in parts:
        for group in range(8):
            copy_in(place + group, source, group).start()

    for place, source in parts:

        def body(group, carry, place=place, source=source):
            copy_in(place + group, source, group).wait()
            backward_maps(state_ref.at[place + group], units_ref.at[place + group])
            copy_out(units_ref, units_hbm, out_sems, place + group).start()
            return carry

        lax.fori_loop(0, 8, body, 0)
    for group in range(16):
        copy_out(units_ref, units_hbm, out_sems, group).wait()


def dot(a, b):
    return jnp.dot(a, b, preferred_element_type=jnp.float32)


def dot_nt(a, b):
    return lax.dot_general(a, b, (((1,), (1,)), ((), ())), preferred_element_type=jnp.float32)


def split(x, parts):
    result = []
    for _ in range(parts):
        result.append(x.astype(jnp.bfloat16))
        x = x - result[-1].astype(jnp.float32)
    return result


def product3(a, b):
    (ah, al), (bh, bl) = a, b
    return dot(ah, bh) + (dot(ah, bl) + dot(al, bh))


def thin_exact(a, b, product=dot):
    high, middle, low = split(a, 3)
    first = product(jnp.concatenate([high, middle, low], axis=0), b[0])
    second = product(jnp.concatenate([high, middle], axis=0), b[1])
    third = product(high, b[2])
    small = first[32:48] + second[16:32] + third
    return first[:16] + (first[16:32] + second[:16] + small)


def thin_near(a, b):
    high, middle = split(a, 2)
    first = dot(jnp.concatenate([high, middle], axis=0), b[0])
    return first[:16] + (first[16:] + dot(high, b[1]))


def merge_blocks(lines, block):
    total = pick_blocks(lines, block)
    for d in range(1, FOUR):
        moved = pick_blocks([lines[(k - d) % FOUR] for k in range(FOUR)], block)
        total = total + pltpu.roll(moved, LANES - SIDE * d, 1)
    return total


def image_stencil(lines, masks, block):
    lines = [across(x, *masks) for x in lines]
    ups = [pltpu.roll(x, SIDE, 1) for x in lines]
    downs = [pltpu.roll(x, LANES - SIDE, 1) for x in lines]
    zero = jnp.zeros_like(lines[0])
    result = []
    for s in range(8):
        up = jnp.where(block == 0, ups[s - 1] if s else zero, ups[s])
        down = jnp.where(block == 3, downs[s + 1] if s < 7 else zero, downs[s])
        result.append(lines[s] + up + down)
    return result


def solve_kernel(
    own_ref,
    other_ref,
    support_labels_hbm,
    columns_ref,
    pack_hbm,
    units_hbm,
    state_t_hbm,
    state_s_hbm,
    grad_hbm,
    objective_ref,
    support_labels_ref,
    grad_ref,
    inverses_ref,
    units_ref,
    second_ref,
    kernel_ref,
    inverse_ref,
    matrix_parts,
    cross_parts,
    inverse_parts,
    weights_ref,
    grads_ref,
    sems,
):
    core = lax.axis_index("sup") % 2
    copies = [
        pltpu.make_async_copy(source, target, sems.at[n])
        for n, (source, target) in enumerate(
            [
                (pack_hbm.at[3], inverses_ref.at[0]),
                (pack_hbm.at[5], inverses_ref.at[1]),
                (units_hbm, units_ref),
                (state_t_hbm.at[:, pl.ds(6 * SIDE, SIDE + 12)], second_ref.at[pl.ds(0, 8)]),
                (state_s_hbm.at[:, pl.ds(6 * SIDE, SIDE + 12)], second_ref.at[pl.ds(8, 8)]),
                (support_labels_hbm, support_labels_ref),
            ]
        )
    ]
    for copy in copies:
        copy.start()

    count = 256
    for half, source_ref in enumerate((own_ref, other_ref)):
        first = 16 * (core if half == 0 else 1 - core)
        for j in range(FOUR):
            for h in range(2):
                blocks = []
                for i in range(FOUR):
                    start = (FOUR * h + i) * 16 * FOUR + j
                    blocks.append(source_ref[pl.ds(start, 16, stride=FOUR), :])
                for b, y in enumerate(turned_blocks(blocks)):
                    start = (FOUR * (b // 2) + j) * 32 + first
                    rows = pl.ds(pl.multiple_of(start, 16), 16)
                    lanes = pl.ds(h * LANES, LANES)
                    if b % 2 == 0:
                        kernel_ref[rows, lanes] = y
                    else:
                        for n, part in enumerate(split(y, 3)):
                            cross_parts[n, rows, lanes] = part

    matrix = kernel_ref[...]
    row_id = lax.broadcasted_iota(jnp.int32, (count, count), 0)
    col_id = lax.broadcasted_iota(jnp.int32, (count, count), 1)
    eye = row_id == col_id
    trace = jnp.sum(jnp.where(eye, matrix, 0.0))
    ridge = 0.1 * trace / count
    matrix = matrix + jnp.where(eye, ridge, 0.0)
    for n, part in enumerate(split(matrix, 3)):
        matrix_parts[n] = part

    def whole(x):
        return jnp.sum(x, axis=1, keepdims=True)

    v_row, v_col = jnp.sum(matrix, axis=0, keepdims=True), whole(matrix)
    norm = lax.rsqrt(whole(v_row * v_row))
    v_row, v_col = v_row * norm, v_col * norm
    w_row, w_col = jnp.sum(matrix * v_col, axis=0, keepdims=True), whole(matrix * v_row)
    top = whole(w_row * v_row)
    off = w_row - top * v_row
    rest = jnp.sum(jnp.abs(matrix - (top * v_col) * v_row), axis=0, keepdims=True)
    rest = jnp.max(rest, axis=1, keepdims=True)
    alpha = 2.0 / (rest + ridge)
    limit = jnp.maximum(alpha * rest, 1.0) + jnp.sqrt(alpha / top * whole(off * off))
    floor = alpha * ridge
    scale = 2.0 / (limit + floor)
    spread = (limit - floor) / (limit + floor)
    square = spread * spread
    gain = 2.0 / (2.0 - square)
    gamma = scale * (1.0 / top - alpha)
    alpha = scale * alpha
    side = gain * ((2.0 * gamma - gamma * gamma * top) * v_col - (alpha * gamma) * w_col)
    inverse_ref[...] = (
        jnp.where(eye, 2.0 * gain * alpha, 0.0)
        - (gain * alpha * alpha) * matrix
        + side * v_row
        - (gain * alpha * gamma * v_col) * w_row
    )
    square = square[0, 0]

    def improve(delta):
        square = delta * delta
        gain = 2.0 / (2.0 - square)
        x = inverse_ref[...]
        parts = split(x, 2)
        error = jnp.where(eye, 1.0, 0.0) - product3((matrix_parts[0], matrix_parts[1]), parts)
        inverse_ref[...] = gain * (x + product3(parts, split(error, 2)))
        return square / (2.0 - square)

    lax.while_loop(lambda delta: delta > 1e-3, improve, square / (2.0 - square))
    for n, part in enumerate(split(inverse_ref[...], 2)):
        inverse_parts[n] = part

    class_id = lax.broadcasted_iota(jnp.int32, (16, count), 0)

    def one_hot(labels):
        hot = (class_id == labels).astype(jnp.float32) - 0.1
        return jnp.where(class_id < CLASSES, hot, 0.0)

    copies[-1].wait()
    natural = jnp.where(
        class_id < CLASSES, (class_id == support_labels_ref[...]).astype(jnp.float32), 0.0
    )
    member = col_id % SIDE
    source = col_id - member + 2 * (member % 16) + member // 16
    support_hot = dot(natural.astype(jnp.bfloat16), (row_id == source).astype(jnp.bfloat16))
    support_hot = jnp.where(class_id < CLASSES, support_hot - 0.1, 0.0)
    lane1 = lane_index((1, LANES))
    halves = []
    for h in range(2):
        line = [columns_ref[pl.ds((FOUR * h + i) * 32 + 24, 1), :] for i in range(FOUR)]
        line = [jnp.where(lane1 // SIDE == i, x, 0.0) for i, x in enumerate(line)]
        halves.append((line[0] + line[1]) + (line[2] + line[3]))
    target_labels = jnp.concatenate(halves, axis=1).astype(jnp.int32)
    target_hot = one_hot(target_labels)

    def refine(coeffs, adjoint):
        step = thin_near(support_hot - thin_exact(coeffs, matrix_parts), inverse_parts)
        coeffs = coeffs + step
        residual = thin_exact(coeffs, cross_parts) - target_hot
        right = thin_exact(residual, cross_parts, dot_nt)
        if adjoint is None:
            adjoint = thin_near(right, inverse_parts)
        more = thin_near(right - thin_exact(adjoint, matrix_parts), inverse_parts)
        adjoint = adjoint + more
        moved = jnp.maximum(
            whole(jnp.sum(step * step, axis=0, keepdims=True))
            / whole(jnp.sum(coeffs * coeffs, axis=0, keepdims=True)),
            whole(jnp.sum(more * more, axis=0, keepdims=True))
            / whole(jnp.sum(adjoint * adjoint, axis=0, keepdims=True)),
        )
        return coeffs, adjoint, residual, moved

    coeffs, adjoint, residual, moved = refine(thin_near(support_hot, inverse_parts), None)

    def again(state):
        coeffs, adjoint, _, moved, _, rounds = state
        coeffs, adjoint, residual, now = refine(coeffs, adjoint)
        return coeffs, adjoint, residual, now, (now * now / moved)[0, 0], rounds + 1

    coeffs, adjoint, residual, _, _, _ = lax.while_loop(
        lambda state: jnp.logical_and(state[4] > 1e-13, state[5] < 40),
        again,
        (coeffs, adjoint, residual, moved, (moved * moved)[0, 0], 0),
    )
    objective_ref[...] = jnp.full((8, LANES), 0.5 * jnp.sum(residual * residual), jnp.float32)
    trace_grad = -jnp.sum(adjoint * coeffs)

    mine_t = lax.axis_index("tgt")
    mine = core * 16 + lax.axis_index("sup") // 2
    coeff_parts, adjoint_parts = split(coeffs, 3), split(adjoint, 3)
    ids = lax.broadcasted_iota(jnp.int32, (16, count), 1)
    wanted = lax.broadcasted_iota(jnp.int32, (16, count), 0) * 32 + mine
    picked = dot_nt(
        (ids == wanted).astype(jnp.bfloat16), jnp.concatenate(coeff_parts + adjoint_parts, axis=0)
    ).astype(jnp.bfloat16)
    turn = lax.rem(count - 32 * mine_t, count)

    def row_parts(x):
        return split(pltpu.roll(x, turn, 1)[:, :LANES], 3)

    zero = jnp.zeros((48, LANES), jnp.bfloat16)
    pairs = 0.0
    for c, a, r in zip(row_parts(-coeffs), row_parts(-adjoint), row_parts(residual)):
        side_s = jnp.concatenate([a, a, a, c, c, c], axis=0)
        side_t = jnp.concatenate([r, r, r, zero], axis=0)
        pairs = pairs + dot(picked, jnp.concatenate([side_s, side_t], axis=1))
    sub8 = lax.broadcasted_iota(jnp.int32, (8, LANES), 0)
    lane8 = lane_index((8, LANES))
    own = jnp.logical_and(sub8 == mine_t, lane8 == mine)
    pairs_s = pairs[:8, :LANES] + jnp.where(own, (0.2 / count) * trace_grad, 0.0)
    pairs = jnp.concatenate([pairs[:8, LANES:], pairs_s], axis=0)
    pairs = jnp.where(lane_index((16, LANES)) < SIDE, pairs * (2.0 / 1024.0), 0.0)
    high, middle, low = [part.astype(jnp.float32) for part in split(pairs, 3)]
    stacked = high + pltpu.roll(middle, 32, 1) + pltpu.roll(low, 64, 1)
    widen = lax.broadcasted_iota(jnp.int32, (LANES, 1024), 0) % SIDE
    widen = widen == lax.broadcasted_iota(jnp.int32, (LANES, 1024), 1) // SIDE
    wide = dot(stacked.astype(jnp.bfloat16), widen.astype(jnp.bfloat16))
    for g in range(8):
        weights_ref[g] = wide[:8, g * LANES : (g + 1) * LANES]
        weights_ref[8 + lax.rem(g + FOUR * core, 8)] = wide[8:, g * LANES : (g + 1) * LANES]

    for copy in copies[:-1]:
        copy.wait()

    block = lane8 // SIDE

    def gather_line(s, carry):
        lines = [[] for _ in range(5)]
        for k in range(FOUR):
            r = s * FOUR + k
            sums = [None] * 5
            for g in range(16):
                weight = weights_ref[g]
                dx = weight * units_ref[g, r]
                terms = [
                    dx
                    * jnp.broadcast_to(
                        second_ref[g, SIDE + FOUR * c + k, pl.ds(s, 1), :], (8, LANES)
                    )
                    for c in range(3)
                ]
                terms.append(weight * units_ref[g, SIDE + r])
                terms.append(weight * second_ref[g, r])
                sums = [t if a is None else a + t for a, t in zip(sums, terms)]
            for n in range(5):
                lines[n].append(sums[n])
        for n in range(5):
            grads_ref[n, s] = merge_blocks(lines[n], block)
        return carry

    lax.fori_loop(0, 8, gather_line, 0, unroll=8)

    masks = edge_masks((8, LANES))

    def half_over_variance(n, s):
        inverse = pick_blocks([inverses_ref[n, FOUR * s + k] for k in range(FOUR)], block)
        return 0.5 * inverse * inverse

    second = [half_over_variance(1, s) * grads_ref[4, s] for s in range(8)]
    second = image_stencil(second, masks, block)
    first = [
        half_over_variance(0, s) * grads_ref[3, s] + (0.5 * SECOND) * second[s] for s in range(8)
    ]
    first = image_stencil(first, masks, block)
    for s in range(8):
        for c in range(3):
            image = columns_ref[pl.ds(c * 8 + s, 8, stride=32), :]
            grad_ref[pl.ds(c * 8 + s, 8, stride=24), :] = (
                grads_ref[c, s] + (2.0 * FIRST) * first[s] * image
            )
    copy = pltpu.make_async_copy(grad_ref, grad_hbm, sems.at[6])
    copy.start()
    copy.wait()


def f32(*shape):
    return jax.ShapeDtypeStruct(shape, jnp.float32)


HBM = pl.BlockSpec(memory_space=pltpu.HBM)
VMEM = pl.BlockSpec(memory_space=pltpu.VMEM)


def call(kernel, ins, outs, shapes, scratch, limit, work=0):
    return pl.pallas_call(
        kernel,
        in_specs=ins,
        out_specs=outs,
        out_shape=shapes,
        scratch_shapes=scratch,
        compiler_params=pltpu.CompilerParams(vmem_limit_bytes=limit * KIB),
        cost_estimate=pl.CostEstimate(flops=work, bytes_accessed=4 << 20, transcendentals=0),
    )


PLANES = (8, 7, FOUR, 8, LANES)
STATE = (8, MAPS + 12, 8, LANES)
UNITS = (16, 2 * SIDE, 8, LANES)
PACK = (7, SIDE, 8, LANES)
WORK = 256 * 1024 * 140


def spread(x, axes, pieces, **groups):
    moved = lax.all_to_all(x.reshape(pieces, -1), axes, 0, 0, tiled=True, **groups)
    return moved.reshape(x.shape)


def on_device(support, support_labels, targets, target_labels):
    scratch = pltpu.VMEM
    zx = [[2 * m + core for m in range(16)] for core in range(2)]
    chips = [[2 * chip + core for chip in range(128)] for core in range(2)]
    cores = [(device, device ^ 1) for device in range(32)]

    image = support.reshape(24, LANES)
    column_message, row_message = call(
        message_kernel, [VMEM] * 2, [VMEM] * 2, [f32(8, 32, LANES), f32(16, 24, LANES)], [], 60 * KIB
    )(image, target_labels.reshape(1, 32))
    columns = lax.all_to_all(column_message, "tgt", 0, 0, tiled=True).reshape(256, LANES)
    planes_t = call(row_kernel, [VMEM], VMEM, f32(*PLANES), [], 48 * KIB, WORK // 2)(
        targets.transpose(1, 0, 2)
    )
    columns, planes_t, row_message = lax.optimization_barrier((columns, planes_t, row_message))
    rows = lax.all_to_all(row_message, "sup", 0, 0, tiled=True, axis_index_groups=zx)
    entries_t, pack, state_t = call(
        target_kernel,
        [VMEM] * 2,
        [VMEM] * 2 + [HBM],
        [f32(8, LANES), f32(*PACK), f32(*STATE)],
        [
            scratch(STATE, jnp.float32),
            scratch((8, 1024), jnp.float32),
            pltpu.SemaphoreType.DMA((8,)),
        ],
        51500,
        WORK,
    )(planes_t, columns)
    rows, entries_t = lax.optimization_barrier((rows, entries_t))
    rows_other = lax.ppermute(rows, "sup", cores)
    planes_own = call(
        half_kernel, [VMEM], VMEM, f32(FOUR, *PLANES[1:]), [], 48 * KIB, WORK // 2
    )(rows)
    payload, state_s = call(
        entries_kernel,
        [VMEM] * 4,
        [HBM] * 2,
        [f32(512, LANES), f32(*STATE)],
        [
            scratch((FOUR, *PLANES[1:]), jnp.float32),
            scratch(STATE, jnp.float32),
            scratch((8, 1024), jnp.float32),
            scratch((512, LANES), jnp.float32),
            pltpu.SemaphoreType.DMA((9,)),
        ],
        52500,
        WORK // 2,
    )(planes_own, rows_other, pack, entries_t)
    received = spread(payload, BOTH, 128, axis_index_groups=chips)
    units = call(
        units_kernel,
        [HBM] * 2,
        HBM,
        f32(*UNITS),
        [
            scratch((16, 6 * SIDE, 8, LANES), jnp.float32),
            scratch(UNITS, jnp.float32),
            pltpu.SemaphoreType.DMA((16,)),
            pltpu.SemaphoreType.DMA((16,)),
        ],
        54200,
        WORK,
    )(state_t, state_s)
    received, units = lax.optimization_barrier((received, units))
    received_other = lax.ppermute(received, "sup", cores)
    partial, objective = call(
        solve_kernel,
        [VMEM] * 2 + [HBM, VMEM] + [HBM] * 4,
        [HBM, VMEM],
        [f32(192, LANES), f32(8, LANES)],
        [
            scratch((1, 256), jnp.int32),
            scratch((192, LANES), jnp.float32),
            scratch((2, SIDE, 8, LANES), jnp.float32),
            scratch((16, 2 * SIDE, 8, LANES), jnp.float32),
            scratch((16, SIDE + 12, 8, LANES), jnp.float32),
            scratch((256, 256), jnp.float32),
            scratch((256, 256), jnp.float32),
            scratch((3, 256, 256), jnp.bfloat16),
            scratch((3, 256, 256), jnp.bfloat16),
            scratch((2, 256, 256), jnp.bfloat16),
            scratch((16, 8, LANES), jnp.float32),
            scratch((5, 8, 8, LANES), jnp.float32),
            pltpu.SemaphoreType.DMA((7,)),
        ],
        54200,
        WORK,
    )(
        received,
        received_other,
        support_labels.reshape(1, 256),
        columns,
        pack,
        units,
        state_t,
        state_s,
    )
    pieces = lax.all_to_all(partial.reshape(8, 24, LANES), "tgt", 0, 0, tiled=True)
    return jnp.sum(pieces, axis=0).reshape(1, 3, 1024), objective[0, 0]


def solution(mesh):
    placed = (P(BOTH, None, None), P(), P("tgt", None, None), P("tgt"))
    return jax.shard_map(
        on_device,
        mesh=mesh,
        in_specs=placed,
        out_specs=(P(BOTH, None, None), P()),
        check_vma=False,
    )
```

```python
import functools
import math

import jax
import jax.numpy as jnp
from jax import lax
from jax.experimental import pallas as pl
from jax.experimental.pallas import tpu as pltpu
from jax.sharding import PartitionSpec as P

SIDE = 32
CLASSES = 10
BOTH = ("tgt", "sup")
LANES = 128
MAPS = 7 * 32
FOUR = 4
ALPHA1 = (2.0 / 9.0) / (2.0 * math.pi)
ALPHA2 = 1.0 / (2.0 * math.pi)
FIRST = 2.0 / 27.0
SECOND = 2.0 / 9.0
ACOS = (
    1.570796238860342,
    -0.21459108884050843,
    0.08883588680709523,
    -0.04919743925456755,
    0.027762915193263623,
    -0.01200339464235187,
    0.002611719889929782,
)
KIB = 1024
HIGHEST = lax.Precision.HIGHEST


def lane_index(shape):
    return lax.broadcasted_iota(jnp.int32, shape, len(shape) - 1)


def across(x, keep_left, keep_right):
    axis = x.ndim - 1
    return x + pltpu.roll(x, 1, axis) * keep_left + pltpu.roll(x, LANES - 1, axis) * keep_right


def edge_masks(shape):
    column = lane_index(shape) % SIDE
    return (column != 0).astype(jnp.float32), (column != SIDE - 1).astype(jnp.float32)


def pick_blocks(lines, block):
    low = jnp.where(block == 0, lines[0], lines[1])
    return jnp.where(block < 2, low, jnp.where(block == 2, lines[2], lines[3]))


def turned_blocks(lines):
    block = lane_index(lines[0].shape) // SIDE
    result = []
    for k in range(FOUR):
        y = pick_blocks([lines[(p - k) % FOUR] for p in range(FOUR)], block)
        result.append(pltpu.roll(y, LANES - SIDE * k, y.ndim - 1) if k else y)
    return result


def spread_blocks(y):
    lane = lane_index(y.shape)
    low = lane < 64
    even = (lane // SIDE) % 2 == 0
    axis = y.ndim - 1
    turned = pltpu.roll(y, 64, axis)
    first = jnp.where(low, y, turned)
    last = jnp.where(low, turned, y)
    first_turned = pltpu.roll(first, 32, axis)
    last_turned = pltpu.roll(last, 32, axis)
    return (
        jnp.where(even, first, first_turned),
        jnp.where(even, first_turned, first),
        jnp.where(even, last, last_turned),
        jnp.where(even, last_turned, last),
    )


def message_kernel(image_ref, labels_ref, column_ref, row_ref):
    hot = labels_ref[...].astype(jnp.float32)
    labels = jnp.broadcast_to(jnp.concatenate([hot] * FOUR, axis=1), (8, LANES))
    image = image_ref[...]
    for d in range(column_ref.shape[0]):
        column_ref[d, pl.ds(0, 24), :] = image
        column_ref[d, pl.ds(24, 8), :] = labels
    turned = pltpu.roll(image, SIDE * (lax.axis_index("sup") // 2 % FOUR), 1)
    for d in range(row_ref.shape[0]):
        row_ref[d] = turned


def column_maps(images_ref, pack_ref):
    keep_left, keep_right = edge_masks((8, LANES))
    for c in range(3):
        for s in range(8):
            y = images_ref[pl.ds(c * 8 + s, 8, stride=32), :]
            for k, z in enumerate(spread_blocks(y)):
                pack_ref[c, 4 * s + k] = z
    sums, variances = {}, {}
    for r in range(SIDE):
        b0, b1, b2 = pack_ref[0, r], pack_ref[1, r], pack_ref[2, r]
        sums[r] = across(b0 * b0 + b1 * b1 + b2 * b2, keep_left, keep_right)
    for r in range(SIDE):
        q = FIRST * vertical(sums, r) + 0.1
        inverse = lax.rsqrt(q)
        pack_ref[3, r] = inverse
        pack_ref[4, r] = q * inverse
        variances[r] = across(q, keep_left, keep_right)
    for r in range(SIDE):
        q = (0.5 * SECOND) * vertical(variances, r) + 0.1
        inverse = lax.rsqrt(q)
        pack_ref[5, r] = inverse
        pack_ref[6, r] = q * inverse


def row_maps(images, rows_ref):
    keep_left, keep_right = edge_masks((8, LANES))
    sublane = lax.broadcasted_iota(jnp.int32, (8, LANES), 0)

    def down(planes):
        above = jnp.where(sublane == 0, 0.0, pltpu.roll(planes[FOUR - 1], 1, 0))
        under = jnp.where(sublane == 7, 0.0, pltpu.roll(planes[0], 7, 0))
        line = [above, *planes, under]
        return [line[k] + line[k + 1] + line[k + 2] for k in range(FOUR)]

    squares = [0.0] * FOUR
    for c in range(3):
        planes = turned_blocks([images(i, c) for i in range(FOUR)])
        for k in range(FOUR):
            rows_ref[c, k] = FIRST * planes[k]
            squares[k] = squares[k] + planes[k] * planes[k]
    squares = [across(x, keep_left, keep_right) for x in squares]
    first = [FIRST * t + 0.1 for t in down(squares)]
    second = [
        (0.5 * SECOND) * t + 0.1 for t in down([across(q, keep_left, keep_right) for q in first])
    ]
    for k in range(FOUR):
        for n, q in ((3, first[k]), (5, second[k])):
            inverse = lax.rsqrt(q)
            rows_ref[n, k] = inverse
            rows_ref[n + 1, k] = q * inverse


def vertical(window, r):
    total = window[r]
    if r > 0:
        total = total + window[r - 1]
    if r < SIDE - 1:
        total = total + window[r + 1]
    return total


def vertical_pair(window, r, offset=None):
    both = window[r] + window[r + 1]
    if offset is not None:
        both = both + offset
    upper = both + window[r - 1] if r > 0 else both
    lower = both + window[r + 2] if r + 2 < SIDE else both
    return upper, lower


def arc(sigma, inverse, scale, alpha, bump):
    raw = sigma * inverse
    if bump is not None:
        raw = raw + bump
    cosine = jnp.clip(raw, -0.9999, 0.9999)
    inside = cosine == raw
    size = jnp.abs(cosine)
    below = 1.0 - size
    poly = jnp.float32(alpha * ACOS[-1])
    for coefficient in ACOS[-2::-1]:
        poly = poly * size + jnp.float32(alpha * coefficient)
    angle = (below * lax.rsqrt(below)) * poly
    slope = jnp.where(cosine >= 0.0, jnp.float32(alpha * math.pi) - angle, angle)
    rest = 1.0 - cosine * cosine
    root = alpha * lax.rsqrt(rest)
    value = scale * (rest * root + slope * cosine)
    return value, slope, root * inverse, inside


def forward_maps(rows_ref, pack_ref, state_ref, bump):
    keep_left, keep_right = edge_masks((8, LANES))

    def row(c, r):
        return jnp.broadcast_to(rows_ref[c, r % FOUR, pl.ds(r // FOUR, 1), :], (8, LANES))

    cross, value_sum, slope_sum = {}, {}, {}
    total = jnp.zeros((8, LANES), jnp.float32)
    for step in range(0, SIDE + 6, 2):
        for r in (step, step + 1):
            if r < SIDE:
                x = row(0, r) * pack_ref[0, r] + row(1, r) * pack_ref[1, r]
                x = x + row(2, r) * pack_ref[2, r]
                cross[r] = across(x, keep_left, keep_right)
        base = step - 2
        if 0 <= base < SIDE:
            for r, sigma in zip((base, base + 1), vertical_pair(cross, base, 0.1)):
                inverse = row(3, r) * pack_ref[3, r]
                scale = row(4, r) * pack_ref[4, r]
                value, slope, weight, inside = arc(sigma, inverse, scale, ALPHA1, None)
                product = slope * sigma
                value_sum[r] = across(value, keep_left, keep_right)
                slope_sum[r] = across(product, keep_left, keep_right)
                state_ref[r] = sigma
                state_ref[SIDE + r] = value
                state_ref[2 * SIDE + r] = jnp.where(inside, slope, -slope)
                state_ref[3 * SIDE + r] = jnp.where(inside, sigma * weight, 0.0)
        base = step - 4
        if 0 <= base < SIDE:
            for r, sigma, more in zip(
                (base, base + 1),
                vertical_pair(value_sum, base, 0.1),
                vertical_pair(slope_sum, base),
            ):
                theta = sigma + more
                inverse = row(5, r) * pack_ref[5, r]
                scale = row(6, r) * pack_ref[6, r]
                value, slope, weight, inside = arc(sigma, inverse, scale, ALPHA2, bump)
                total = total + (value + slope * theta)
                dsigma = jnp.where(inside, slope + theta * weight, 0.0)
                state_ref[4 * SIDE + r] = slope
                state_ref[5 * SIDE + r] = dsigma + slope
                state_ref[6 * SIDE + r] = value - dsigma * sigma
    return total


def backward_maps(state_ref, units_ref):
    keep_left, keep_right = edge_masks((8, LANES))
    dslope, dsigma, dtheta = {}, {}, {}
    for step in range(0, SIDE + 6, 2):
        for r in (step, step + 1):
            if r < SIDE:
                dslope[r] = across(state_ref[4 * SIDE + r], keep_left, keep_right)
                dsigma[r] = across(state_ref[5 * SIDE + r], keep_left, keep_right)
        base = step - 2
        if 0 <= base < SIDE:
            for r, dvalue, dproduct in zip(
                (base, base + 1), vertical_pair(dsigma, base), vertical_pair(dslope, base)
            ):
                slope = state_ref[2 * SIDE + r]
                inner = jnp.maximum(slope, 0.0) * dvalue + dproduct * state_ref[3 * SIDE + r]
                squeeze = state_ref[SIDE + r] * dvalue - inner * state_ref[r]
                units_ref[SIDE + r] = squeeze
                dtheta[r] = across(inner + dproduct * jnp.abs(slope), keep_left, keep_right)
        base = step - 4
        if 0 <= base < SIDE:
            for r, unit in zip((base, base + 1), vertical_pair(dtheta, base)):
                units_ref[r] = unit


def sum_entries(totals_ref):
    parts = [part.astype(jnp.float32) for part in split(totals_ref[...] * (2.0 / 1024.0), 3)]
    stacked = jnp.concatenate(parts + [jnp.zeros((8, 1024), jnp.float32)], axis=0)
    source = lax.broadcasted_iota(jnp.int32, (1024, LANES), 0) // SIDE
    pick = (source == lane_index((1024, LANES))).astype(jnp.bfloat16)
    sums = dot(stacked.astype(jnp.bfloat16), pick)
    return sums[:8] + (sums[8:16] + sums[16:24])


def keep_total(totals_ref, group, total):
    totals_ref[:, pl.ds(pl.multiple_of(group * LANES, LANES), LANES)] = total


def keep_planes(planes_ref, group, state_ref, place):
    for c in range(3):
        for k in range(FOUR):
            state_ref[place, MAPS + FOUR * c + k] = planes_ref[group, c, k]


def own_bump(group):
    image = group * FOUR + lane_index((8, LANES)) // SIDE
    column = lax.broadcasted_iota(jnp.int32, (8, LANES), 0)
    mine = lax.axis_index("sup") // 2
    own = jnp.logical_and(image == mine, column == lax.axis_index("tgt"))
    return own.astype(jnp.float32)


def copy_out(units_ref, units_hbm, sems, group):
    return pltpu.make_async_copy(units_ref.at[group], units_hbm.at[group], sems.at[group])


def row_kernel(images_ref, planes_ref):
    for group in range(8):

        def image(i, c, group=group):
            n = group * FOUR + i
            lines = [images_ref[c, pl.ds(n, 1), pl.ds(s * LANES, LANES)] for s in range(8)]
            x = jnp.concatenate(lines, axis=0)
            return pltpu.roll(x, SIDE * i, 1) if i else x

        row_maps(image, planes_ref.at[group])


def target_kernel(
    planes_ref,
    columns_ref,
    entries_ref,
    pack_ref,
    state_hbm,
    state_ref,
    totals_ref,
    sems,
):
    column_maps(columns_ref, pack_ref)

    def body(group, carry):
        total = forward_maps(planes_ref.at[group], pack_ref, state_ref.at[group], None)
        keep_total(totals_ref, group, total)
        keep_planes(planes_ref, group, state_ref, group)
        copy_out(state_ref, state_hbm, sems, group).start()
        return carry

    lax.fori_loop(0, 8, body, 0)
    entries_ref[...] = sum_entries(totals_ref)
    for group in range(8):
        copy_out(state_ref, state_hbm, sems, group).wait()


def half_kernel(images_ref, planes_ref):
    for group in range(FOUR):
        row_maps(
            lambda i, c: images_ref[group * FOUR + i, pl.ds(c * 8, 8), :], planes_ref.at[group]
        )


def own_kernel(images_ref, pack_ref, planes_ref, state_ref, total_ref):
    half_kernel(images_ref, planes_ref)
    total_ref[...] = forward_maps(planes_ref.at[0], pack_ref, state_ref.at[0], own_bump(0))
    keep_planes(planes_ref, 0, state_ref, 0)


def entries_kernel(
    planes_own_ref,
    first_state_ref,
    first_total_ref,
    other_ref,
    pack_ref,
    entries_t_ref,
    payload_hbm,
    state_hbm,
    planes_ref,
    state_ref,
    totals_ref,
    payload_ref,
    sems,
):
    first_out = copy_out(first_state_ref, state_hbm, sems, 0)
    first_out.start()
    totals_ref[:, :LANES] = first_total_ref[...]
    half_kernel(other_ref, planes_ref)

    def own_body(group, carry):
        total = forward_maps(
            planes_own_ref.at[group], pack_ref, state_ref.at[group], own_bump(group)
        )
        keep_total(totals_ref, group, total)
        keep_planes(planes_own_ref, group, state_ref, group)
        copy_out(state_ref, state_hbm, sems, group).start()
        return carry

    def other_body(group, carry):
        place = FOUR + group
        total = forward_maps(planes_ref.at[group], pack_ref, state_ref.at[place], None)
        keep_total(totals_ref, place, total)
        keep_planes(planes_ref, group, state_ref, place)
        copy_out(state_ref, state_hbm, sems, place).start()
        return carry

    lax.fori_loop(1, FOUR, own_body, 0)
    lax.fori_loop(0, FOUR, other_body, 0)
    entries = sum_entries(totals_ref)
    lane = lane_index((8, LANES))
    turned = jnp.where(lane < 16, pltpu.roll(entries, LANES - 16, 1), pltpu.roll(entries, 16, 1))
    turned = jnp.where(lane < SIDE, turned, 0.0)
    entries = jnp.where(lax.axis_index("sup") % 2 == 1, turned, entries)
    both = entries + pltpu.roll(entries_t_ref[...], SIDE, 1)
    both = both + pltpu.roll(pltpu.roll(both, 64, 1), FOUR, 0)
    both = pltpu.roll(both, SIDE * (lax.axis_index("tgt") % FOUR), 1)
    both = jnp.concatenate([both[:FOUR], both[:FOUR]], axis=0)
    for d in range(payload_ref.shape[0] // 8):
        payload_ref[pl.ds(8 * d, 8), :] = both
    payload_out = pltpu.make_async_copy(payload_ref, payload_hbm, sems.at[8])
    payload_out.start()
    for group in range(8):
        copy_out(state_ref, state_hbm, sems, group).wait()
    payload_out.wait()


def units_kernel(state_t_hbm, state_s_hbm, units_hbm, state_ref, units_ref, in_sems, out_sems):
    def copy_in(place, source, group):
        return pltpu.make_async_copy(
            source.at[group, pl.ds(0, 6 * SIDE)], state_ref.at[place], in_sems.at[place]
        )

    parts = ((0, state_t_hbm), (8, state_s_hbm))
    for place, source in parts:
        for group in range(8):
            copy_in(place + group, source, group).start()

    for place, source in parts:

        def body(group, carry, place=place, source=source):
            copy_in(place + group, source, group).wait()
            backward_maps(state_ref.at[place + group], units_ref.at[place + group])
            copy_out(units_ref, units_hbm, out_sems, place + group).start()
            return carry

        lax.fori_loop(0, 8, body, 0)
    for group in range(16):
        copy_out(units_ref, units_hbm, out_sems, group).wait()


def dot(a, b):
    return jnp.dot(a, b, preferred_element_type=jnp.float32)


def dot_nt(a, b):
    return lax.dot_general(a, b, (((1,), (1,)), ((), ())), preferred_element_type=jnp.float32)


def split(x, parts):
    result = []
    for _ in range(parts):
        result.append(x.astype(jnp.bfloat16))
        x = x - result[-1].astype(jnp.float32)
    return result


def product3(a, b):
    (ah, al), (bh, bl) = a, b
    return dot(ah, bh) + (dot(ah, bl) + dot(al, bh))


def thin_exact(a, b, product=dot):
    high, middle, low = split(a, 3)
    first = product(jnp.concatenate([high, middle, low], axis=0), b[0])
    second = product(jnp.concatenate([high, middle], axis=0), b[1])
    third = product(high, b[2])
    small = first[32:48] + second[16:32] + third
    return first[:16] + (first[16:32] + second[:16] + small)


def thin_near(a, b):
    high, middle = split(a, 2)
    first = dot(jnp.concatenate([high, middle], axis=0), b[0])
    return first[:16] + (first[16:] + dot(high, b[1]))


def merge_blocks(lines, block):
    total = pick_blocks(lines, block)
    for d in range(1, FOUR):
        moved = pick_blocks([lines[(k - d) % FOUR] for k in range(FOUR)], block)
        total = total + pltpu.roll(moved, LANES - SIDE * d, 1)
    return total


def image_stencil(lines, masks, block):
    lines = [across(x, *masks) for x in lines]
    ups = [pltpu.roll(x, SIDE, 1) for x in lines]
    downs = [pltpu.roll(x, LANES - SIDE, 1) for x in lines]
    zero = jnp.zeros_like(lines[0])
    result = []
    for s in range(8):
        up = jnp.where(block == 0, ups[s - 1] if s else zero, ups[s])
        down = jnp.where(block == 3, downs[s + 1] if s < 7 else zero, downs[s])
        result.append(lines[s] + up + down)
    return result


def solve_kernel(
    own_ref,
    other_ref,
    support_labels_hbm,
    columns_ref,
    pack_hbm,
    units_hbm,
    state_t_hbm,
    state_s_hbm,
    grad_hbm,
    objective_ref,
    support_labels_ref,
    grad_ref,
    inverses_ref,
    units_ref,
    second_ref,
    kernel_ref,
    inverse_ref,
    matrix_parts,
    cross_parts,
    inverse_parts,
    weights_ref,
    grads_ref,
    sems,
):
    core = lax.axis_index("sup") % 2
    copies = [
        pltpu.make_async_copy(source, target, sems.at[n])
        for n, (source, target) in enumerate(
            [
                (pack_hbm.at[3], inverses_ref.at[0]),
                (pack_hbm.at[5], inverses_ref.at[1]),
                (units_hbm, units_ref),
                (state_t_hbm.at[:, pl.ds(6 * SIDE, SIDE + 12)], second_ref.at[pl.ds(0, 8)]),
                (state_s_hbm.at[:, pl.ds(6 * SIDE, SIDE + 12)], second_ref.at[pl.ds(8, 8)]),
                (support_labels_hbm, support_labels_ref),
            ]
        )
    ]
    for copy in copies:
        copy.start()

    count = 256
    for half, source_ref in enumerate((own_ref, other_ref)):
        first = 16 * (core if half == 0 else 1 - core)
        for j in range(FOUR):
            for h in range(2):
                blocks = []
                for i in range(FOUR):
                    start = (FOUR * h + i) * 16 * FOUR + j
                    blocks.append(source_ref[pl.ds(start, 16, stride=FOUR), :])
                for b, y in enumerate(turned_blocks(blocks)):
                    start = (FOUR * (b // 2) + j) * 32 + first
                    rows = pl.ds(pl.multiple_of(start, 16), 16)
                    lanes = pl.ds(h * LANES, LANES)
                    if b % 2 == 0:
                        kernel_ref[rows, lanes] = y
                    else:
                        for n, part in enumerate(split(y, 3)):
                            cross_parts[n, rows, lanes] = part

    matrix = kernel_ref[...]
    row_id = lax.broadcasted_iota(jnp.int32, (count, count), 0)
    col_id = lax.broadcasted_iota(jnp.int32, (count, count), 1)
    eye = row_id == col_id
    trace = jnp.sum(jnp.where(eye, matrix, 0.0))
    ridge = 0.1 * trace / count
    matrix = matrix + jnp.where(eye, ridge, 0.0)
    for n, part in enumerate(split(matrix, 3)):
        matrix_parts[n] = part

    def whole(x):
        return jnp.sum(x, axis=1, keepdims=True)

    v_row, v_col = jnp.sum(matrix, axis=0, keepdims=True), whole(matrix)
    norm = lax.rsqrt(whole(v_row * v_row))
    v_row, v_col = v_row * norm, v_col * norm
    w_row, w_col = jnp.sum(matrix * v_col, axis=0, keepdims=True), whole(matrix * v_row)
    top = whole(w_row * v_row)
    off = w_row - top * v_row
    rest = jnp.sum(jnp.abs(matrix - (top * v_col) * v_row), axis=0, keepdims=True)
    rest = jnp.max(rest, axis=1, keepdims=True)
    alpha = 2.0 / (rest + ridge)
    limit = jnp.maximum(alpha * rest, 1.0) + jnp.sqrt(alpha / top * whole(off * off))
    floor = alpha * ridge
    scale = 2.0 / (limit + floor)
    spread = (limit - floor) / (limit + floor)
    square = spread * spread
    gain = 2.0 / (2.0 - square)
    gamma = scale * (1.0 / top - alpha)
    alpha = scale * alpha
    side = gain * ((2.0 * gamma - gamma * gamma * top) * v_col - (alpha * gamma) * w_col)
    inverse_ref[...] = (
        jnp.where(eye, 2.0 * gain * alpha, 0.0)
        - (gain * alpha * alpha) * matrix
        + side * v_row
        - (gain * alpha * gamma * v_col) * w_row
    )
    square = square[0, 0]

    def improve(delta):
        square = delta * delta
        gain = 2.0 / (2.0 - square)
        x = inverse_ref[...]
        parts = split(x, 2)
        error = jnp.where(eye, 1.0, 0.0) - product3((matrix_parts[0], matrix_parts[1]), parts)
        inverse_ref[...] = gain * (x + product3(parts, split(error, 2)))
        return square / (2.0 - square)

    lax.while_loop(lambda delta: delta > 1e-3, improve, square / (2.0 - square))
    for n, part in enumerate(split(inverse_ref[...], 2)):
        inverse_parts[n] = part

    class_id = lax.broadcasted_iota(jnp.int32, (16, count), 0)

    def one_hot(labels):
        hot = (class_id == labels).astype(jnp.float32) - 0.1
        return jnp.where(class_id < CLASSES, hot, 0.0)

    copies[-1].wait()
    natural = jnp.where(
        class_id < CLASSES, (class_id == support_labels_ref[...]).astype(jnp.float32), 0.0
    )
    member = col_id % SIDE
    source = col_id - member + 2 * (member % 16) + member // 16
    support_hot = dot(natural.astype(jnp.bfloat16), (row_id == source).astype(jnp.bfloat16))
    support_hot = jnp.where(class_id < CLASSES, support_hot - 0.1, 0.0)
    lane1 = lane_index((1, LANES))
    halves = []
    for h in range(2):
        line = [columns_ref[pl.ds((FOUR * h + i) * 32 + 24, 1), :] for i in range(FOUR)]
        line = [jnp.where(lane1 // SIDE == i, x, 0.0) for i, x in enumerate(line)]
        halves.append((line[0] + line[1]) + (line[2] + line[3]))
    target_labels = jnp.concatenate(halves, axis=1).astype(jnp.int32)
    target_hot = one_hot(target_labels)

    def refine(coeffs, adjoint):
        step = thin_near(support_hot - thin_exact(coeffs, matrix_parts), inverse_parts)
        coeffs = coeffs + step
        residual = thin_exact(coeffs, cross_parts) - target_hot
        right = thin_exact(residual, cross_parts, dot_nt)
        if adjoint is None:
            adjoint = thin_near(right, inverse_parts)
        more = thin_near(right - thin_exact(adjoint, matrix_parts), inverse_parts)
        adjoint = adjoint + more
        moved = jnp.maximum(
            whole(jnp.sum(step * step, axis=0, keepdims=True))
            / whole(jnp.sum(coeffs * coeffs, axis=0, keepdims=True)),
            whole(jnp.sum(more * more, axis=0, keepdims=True))
            / whole(jnp.sum(adjoint * adjoint, axis=0, keepdims=True)),
        )
        return coeffs, adjoint, residual, moved

    coeffs, adjoint, residual, moved = refine(thin_near(support_hot, inverse_parts), None)

    def again(state):
        coeffs, adjoint, _, moved, _, rounds = state
        coeffs, adjoint, residual, now = refine(coeffs, adjoint)
        return coeffs, adjoint, residual, now, (now * now / moved)[0, 0], rounds + 1

    coeffs, adjoint, residual, _, _, _ = lax.while_loop(
        lambda state: jnp.logical_and(state[4] > 1e-13, state[5] < 40),
        again,
        (coeffs, adjoint, residual, moved, (moved * moved)[0, 0], 0),
    )
    objective_ref[...] = jnp.full((8, LANES), 0.5 * jnp.sum(residual * residual), jnp.float32)
    trace_grad = -jnp.sum(adjoint * coeffs)

    mine_t = lax.axis_index("tgt")
    mine = core * 16 + lax.axis_index("sup") // 2
    coeff_parts, adjoint_parts = split(coeffs, 3), split(adjoint, 3)
    ids = lax.broadcasted_iota(jnp.int32, (16, count), 1)
    wanted = lax.broadcasted_iota(jnp.int32, (16, count), 0) * 32 + mine
    picked = dot_nt(
        (ids == wanted).astype(jnp.bfloat16), jnp.concatenate(coeff_parts + adjoint_parts, axis=0)
    ).astype(jnp.bfloat16)
    turn = lax.rem(count - 32 * mine_t, count)

    def row_parts(x):
        return split(pltpu.roll(x, turn, 1)[:, :LANES], 3)

    zero = jnp.zeros((48, LANES), jnp.bfloat16)
    pairs = 0.0
    for c, a, r in zip(row_parts(-coeffs), row_parts(-adjoint), row_parts(residual)):
        side_s = jnp.concatenate([a, a, a, c, c, c], axis=0)
        side_t = jnp.concatenate([r, r, r, zero], axis=0)
        pairs = pairs + dot(picked, jnp.concatenate([side_s, side_t], axis=1))
    sub8 = lax.broadcasted_iota(jnp.int32, (8, LANES), 0)
    lane8 = lane_index((8, LANES))
    own = jnp.logical_and(sub8 == mine_t, lane8 == mine)
    pairs_s = pairs[:8, :LANES] + jnp.where(own, (0.2 / count) * trace_grad, 0.0)
    pairs = jnp.concatenate([pairs[:8, LANES:], pairs_s], axis=0)
    pairs = jnp.where(lane_index((16, LANES)) < SIDE, pairs * (2.0 / 1024.0), 0.0)
    high, middle, low = [part.astype(jnp.float32) for part in split(pairs, 3)]
    stacked = high + pltpu.roll(middle, 32, 1) + pltpu.roll(low, 64, 1)
    widen = lax.broadcasted_iota(jnp.int32, (LANES, 1024), 0) % SIDE
    widen = widen == lax.broadcasted_iota(jnp.int32, (LANES, 1024), 1) // SIDE
    wide = dot(stacked.astype(jnp.bfloat16), widen.astype(jnp.bfloat16))
    for g in range(8):
        weights_ref[g] = wide[:8, g * LANES : (g + 1) * LANES]
        weights_ref[8 + lax.rem(g + FOUR * core, 8)] = wide[8:, g * LANES : (g + 1) * LANES]

    for copy in copies[:-1]:
        copy.wait()

    block = lane8 // SIDE

    def gather_line(s, carry):
        lines = [[] for _ in range(5)]
        for k in range(FOUR):
            r = s * FOUR + k
            sums = [None] * 5
            for g in range(16):
                weight = weights_ref[g]
                dx = weight * units_ref[g, r]
                terms = [
                    dx
                    * jnp.broadcast_to(
                        second_ref[g, SIDE + FOUR * c + k, pl.ds(s, 1), :], (8, LANES)
                    )
                    for c in range(3)
                ]
                terms.append(weight * units_ref[g, SIDE + r])
                terms.append(weight * second_ref[g, r])
                sums = [t if a is None else a + t for a, t in zip(sums, terms)]
            for n in range(5):
                lines[n].append(sums[n])
        for n in range(5):
            grads_ref[n, s] = merge_blocks(lines[n], block)
        return carry

    lax.fori_loop(0, 8, gather_line, 0, unroll=8)

    masks = edge_masks((8, LANES))

    def half_over_variance(n, s):
        inverse = pick_blocks([inverses_ref[n, FOUR * s + k] for k in range(FOUR)], block)
        return 0.5 * inverse * inverse

    second = [half_over_variance(1, s) * grads_ref[4, s] for s in range(8)]
    second = image_stencil(second, masks, block)
    first = [
        half_over_variance(0, s) * grads_ref[3, s] + (0.5 * SECOND) * second[s] for s in range(8)
    ]
    first = image_stencil(first, masks, block)
    for s in range(8):
        for c in range(3):
            image = columns_ref[pl.ds(c * 8 + s, 8, stride=32), :]
            grad_ref[pl.ds(c * 8 + s, 8, stride=24), :] = (
                grads_ref[c, s] + (2.0 * FIRST) * first[s] * image
            )
    copy = pltpu.make_async_copy(grad_ref, grad_hbm, sems.at[6])
    copy.start()
    copy.wait()


def f32(*shape):
    return jax.ShapeDtypeStruct(shape, jnp.float32)


HBM = pl.BlockSpec(memory_space=pltpu.HBM)
VMEM = pl.BlockSpec(memory_space=pltpu.VMEM)


def call(kernel, ins, outs, shapes, scratch, limit, work=0):
    return pl.pallas_call(
        kernel,
        in_specs=ins,
        out_specs=outs,
        out_shape=shapes,
        scratch_shapes=scratch,
        compiler_params=pltpu.CompilerParams(vmem_limit_bytes=limit * KIB),
        cost_estimate=pl.CostEstimate(flops=work, bytes_accessed=4 << 20, transcendentals=0),
    )


PLANES = (8, 7, FOUR, 8, LANES)
STATE = (8, MAPS + 12, 8, LANES)
UNITS = (16, 2 * SIDE, 8, LANES)
PACK = (7, SIDE, 8, LANES)
WORK = 256 * 1024 * 140


def spread(x, axes, pieces, **groups):
    moved = lax.all_to_all(x.reshape(pieces, -1), axes, 0, 0, tiled=True, **groups)
    return moved.reshape(x.shape)


def on_device(support, support_labels, targets, target_labels):
    scratch = pltpu.VMEM
    zx = [[2 * m + core for m in range(16)] for core in range(2)]
    chips = [[2 * chip + core for chip in range(128)] for core in range(2)]
    cores = [(device, device ^ 1) for device in range(32)]

    image = support.reshape(24, LANES)
    column_message, row_message = call(
        message_kernel, [VMEM] * 2, [VMEM] * 2, [f32(8, 32, LANES), f32(16, 24, LANES)], [], 60 * KIB
    )(image, target_labels.reshape(1, 32))
    columns = lax.all_to_all(column_message, "tgt", 0, 0, tiled=True).reshape(256, LANES)
    planes_t = call(row_kernel, [VMEM], VMEM, f32(*PLANES), [], 48 * KIB, WORK // 2)(
        targets.transpose(1, 0, 2)
    )
    columns, planes_t, row_message = lax.optimization_barrier((columns, planes_t, row_message))
    rows = lax.all_to_all(row_message, "sup", 0, 0, tiled=True, axis_index_groups=zx)
    entries_t, pack, state_t = call(
        target_kernel,
        [VMEM] * 2,
        [VMEM] * 2 + [HBM],
        [f32(8, LANES), f32(*PACK), f32(*STATE)],
        [
            scratch(STATE, jnp.float32),
            scratch((8, 1024), jnp.float32),
            pltpu.SemaphoreType.DMA((8,)),
        ],
        51500,
        WORK,
    )(planes_t, columns)
    rows, entries_t = lax.optimization_barrier((rows, entries_t))
    rows_other = lax.ppermute(rows, "sup", cores)
    planes_own, first_state, first_total = call(
        own_kernel,
        [VMEM] * 2,
        [VMEM] * 3,
        [f32(FOUR, *PLANES[1:]), f32(1, *STATE[1:]), f32(8, LANES)],
        [],
        48 * KIB,
        WORK // 2,
    )(rows, pack)
    payload, state_s = call(
        entries_kernel,
        [VMEM] * 6,
        [HBM] * 2,
        [f32(512, LANES), f32(*STATE)],
        [
            scratch((FOUR, *PLANES[1:]), jnp.float32),
            scratch(STATE, jnp.float32),
            scratch((8, 1024), jnp.float32),
            scratch((512, LANES), jnp.float32),
            pltpu.SemaphoreType.DMA((9,)),
        ],
        51400,
        WORK // 2,
    )(planes_own, first_state, first_total, rows_other, pack, entries_t)
    received = spread(payload, BOTH, 128, axis_index_groups=chips)
    units = call(
        units_kernel,
        [HBM] * 2,
        HBM,
        f32(*UNITS),
        [
            scratch((16, 6 * SIDE, 8, LANES), jnp.float32),
            scratch(UNITS, jnp.float32),
            pltpu.SemaphoreType.DMA((16,)),
            pltpu.SemaphoreType.DMA((16,)),
        ],
        54200,
        WORK,
    )(state_t, state_s)
    received, units = lax.optimization_barrier((received, units))
    received_other = lax.ppermute(received, "sup", cores)
    partial, objective = call(
        solve_kernel,
        [VMEM] * 2 + [HBM, VMEM] + [HBM] * 4,
        [HBM, VMEM],
        [f32(192, LANES), f32(8, LANES)],
        [
            scratch((1, 256), jnp.int32),
            scratch((192, LANES), jnp.float32),
            scratch((2, SIDE, 8, LANES), jnp.float32),
            scratch((16, 2 * SIDE, 8, LANES), jnp.float32),
            scratch((16, SIDE + 12, 8, LANES), jnp.float32),
            scratch((256, 256), jnp.float32),
            scratch((256, 256), jnp.float32),
            scratch((3, 256, 256), jnp.bfloat16),
            scratch((3, 256, 256), jnp.bfloat16),
            scratch((2, 256, 256), jnp.bfloat16),
            scratch((16, 8, LANES), jnp.float32),
            scratch((5, 8, 8, LANES), jnp.float32),
            pltpu.SemaphoreType.DMA((7,)),
        ],
        54200,
        WORK,
    )(
        received,
        received_other,
        support_labels.reshape(1, 256),
        columns,
        pack,
        units,
        state_t,
        state_s,
    )
    pieces = lax.all_to_all(partial.reshape(8, 24, LANES), "tgt", 0, 0, tiled=True)
    return jnp.sum(pieces, axis=0).reshape(1, 3, 1024), objective[0, 0]


def solution(mesh):
    placed = (P(BOTH, None, None), P(), P("tgt", None, None), P("tgt"))
    return jax.shard_map(
        on_device,
        mesh=mesh,
        in_specs=placed,
        out_specs=(P(BOTH, None, None), P()),
        check_vma=False,
    )
```
